32 devices in a mesh: section: 2 (over core), seq: 4 (over y, x), mp: 4 (over z).
Axes of the slice: x: 2, y: 2, z: 4, core: 2. Of those that a mesh axis runs over, the one named last changes fastest.
Arguments:
- patches: bfloat16 [4, 256, 1280], P('seq'), may hold values from -50 to 50
- image_place: int32 [4, 4, 16], replicated, may hold values from -1 to 31, as said below
- slot_map: int32 [4, 4], replicated, may hold values from 0 to 15, as said below
- text: bfloat16 [4, 128, 8192], P('seq', ('section', 'mp')), may hold values from -50 to 50
- vision_gain: float32 [1280], replicated, may hold values from 0.25 to 1.75
- qkv_weight: bfloat16 [1280, 3, 1280], P(None, None, ('section', 'mp')), may hold values from -0.15625 to 0.15625
- qkv_bias: float32 [3, 1280], P(None, ('section', 'mp')), may hold values from -4 to 4
- out_weight: bfloat16 [1280, 1280], P(('section', 'mp')), may hold values from -0.625 to 0.625
- out_bias: float32 [1280], replicated, may hold values from -4 to 4
- merge_gain: float32 [1280], replicated, may hold values from 0.25 to 1.75
- merge_up: bfloat16 [5120, 2560], P(None, ('section', 'mp')), may hold values from -0.078125 to 0.078125
- merge_up_bias: float32 [2560], P(('section', 'mp')), may hold values from -4 to 4
- merge_down: bfloat16 [2560, 8192], P(('section', 'mp')), may hold values from -0.125 to 0.125
- merge_down_bias: float32 [8192], replicated, may hold values from -4 to 4
- input_gain: float32 [8192], replicated, may hold values from 0.25 to 1.75
- kv_weight: bfloat16 [8192, 2048], P(None, ('section', 'mp')), may hold values from -0.0625 to 0.0625
- kv_bias: float32 [2048], P(('section', 'mp')), may hold values from -4 to 4
Outputs:
- kv_cache: bfloat16 [2, 16, 32, 1024], P('section', 'seq', None, 'mp')
The draws below stay inside these ranges and needn't reach their ends.
Inputs may be any that keep to these rules, and one draw needn't show every extreme that they name: In every window the units w with image_place >= 0 come first and are at least one; their values are distinct and form a run of consecutive positions; some window has all 16 units placed. slot_map maps the requests one to one onto the slots; the owners slot_map[j, i] // 4 of the 4 requests of any shard j are all different.
All inputs are finite; a program needn't handle non-finite values.
Results may differ from the reference program's by a relative error of at most 0.01.
Values may be sent and summed in bfloat16 or wider, within the bound.
No kernel may reach another device: no remote copies, remote signals or barrier semaphores. Data moves between devices by JAX's collectives and lax.ppermute only.
A program may use at most 128 MiB of HBM per device.

```python
import math
import jax
import jax.numpy as jnp
from jax import lax

D = 8192
KV_HEADS = 8
HEAD = 128
VHEADS = 16
VHEAD = 80
MH = 2560
UNITS = 16
CTX = 32
VD = 1280
WIN = 64
SHARDS = 4
PROMPT = 128
VROWS = 256
SLOTS = 16
HEAD_GROUPS = 8


def scale_field(key, shape, spread):
    first_key, second_key = jax.random.split(key)
    row_scale = jnp.exp(jax.random.uniform(first_key, shape[:-1] + (1,), jnp.float32, 0.0, math.log(spread)))
    column_scale = jnp.exp(jax.random.uniform(second_key, (shape[-1],), jnp.float32, 0.0, math.log(spread)))
    return row_scale * column_scale / spread


def draw_patches(key, part):
    key = jax.random.fold_in(key, 5)
    shape = (SHARDS, VROWS, VD)
    scale_key, base_key = jax.random.split(key, 2)
    base = jax.random.normal(base_key, shape, jnp.float32)
    return (jnp.clip(base, -5.0, 5.0) * scale_field(scale_key, shape, 10.0)).astype(jnp.bfloat16)


def draw_text(key, part):
    key = jax.random.fold_in(key, 7)
    shape = (SHARDS, PROMPT, D)
    scale_key, base_key = jax.random.split(key, 2)
    base = jax.random.normal(base_key, shape, jnp.float32)
    return (jnp.clip(base, -5.0, 5.0) * scale_field(scale_key, shape, 10.0)).astype(jnp.bfloat16)


def draw_image_place(key, part):
    key = jax.random.fold_in(key, 13)
    count_key, offset_key, order_key, full_key = jax.random.split(key, 4)
    counts = jax.random.randint(count_key, (SHARDS, SHARDS), 1, UNITS + 1)
    chosen = jax.random.randint(full_key, (), 0, SHARDS * SHARDS)
    counts = jnp.where(jnp.arange(SHARDS * SHARDS).reshape(SHARDS, SHARDS) == chosen, UNITS, counts)
    offsets = jax.random.randint(offset_key, (SHARDS, SHARDS), 0, CTX - counts + 1)
    order = jax.vmap(lambda sub_key: jax.random.permutation(sub_key, UNITS))(jax.random.split(order_key, SHARDS * SHARDS)).reshape(SHARDS, SHARDS, UNITS)
    unit_ids = jnp.arange(UNITS)
    live = unit_ids[None, None, :] < counts[:, :, None]
    below = (order[:, :, None, :] < order[:, :, :, None]) & live[:, :, None, :]
    ranks = jnp.sum(below.astype(jnp.int32), axis=-1)
    return jnp.where(live, offsets[:, :, None] + ranks, -1).astype(jnp.int32)


def draw_slot_map(key, part):
    key = jax.random.fold_in(key, 17)
    owner_key, seat_key = jax.random.split(key)
    owners = jax.vmap(lambda sub_key: jax.random.permutation(sub_key, SHARDS))(jax.random.split(owner_key, SHARDS))
    seats = jax.vmap(lambda sub_key: jax.random.permutation(sub_key, SHARDS))(jax.random.split(seat_key, SHARDS))
    seat_of = jnp.take_along_axis(seats.T, owners, axis=1)
    return (owners * SHARDS + seat_of).astype(jnp.int32)


def shard_levels(key, dims, cuts, smallest, high):
    level = 1.0
    for dim, shards_of in cuts:
        steps = jax.random.uniform(jax.random.fold_in(jax.random.fold_in(key, 6), dim), (shards_of,), jnp.float32, smallest / len(cuts), high / len(cuts))
        level = level * jnp.repeat(jnp.exp(steps), dims[dim] // shards_of).reshape((-1,) + (1,) * (len(dims) - 1 - dim))
    return level


def centred(stream_key, extent, deviation, reach, pieces=(), kind=jnp.bfloat16):
    result = deviation * jax.random.normal(stream_key, extent, jnp.float32)
    if pieces:
        result = result * shard_levels(stream_key, extent, pieces, -0.22, 0.18)
    return jnp.clip(result, -reach, reach).astype(kind)


def setup_inputs(seed: int = 0) -> dict:
    key_list = jax.random.split(jax.random.key(seed), 18)
    patches = draw_patches(jax.random.fold_in(key_list[17], 71), 0)
    image_place = draw_image_place(jax.random.fold_in(key_list[17], 71), 0)
    slot_map = draw_slot_map(jax.random.fold_in(key_list[17], 71), 0)
    text = draw_text(jax.random.fold_in(key_list[17], 71), 0)
    vision_gain = jnp.clip(1.0 + 0.15 * jax.random.normal(key_list[4], (VD,), jnp.float32), 0.25, 1.75)
    qkv_weight = centred(key_list[5], (VD, 3, VD), VD ** -0.5, 0.15625, ((2, 8),))
    qkv_bias = centred(key_list[6], (3, VD), 0.3, 4.0, ((1, 8),), jnp.float32)
    out_weight = centred(key_list[7], (VD, VD), VHEAD ** -0.5, 0.625, ((0, 8),))
    out_bias = centred(key_list[8], (VD,), 0.3, 4.0, (), jnp.float32)
    merge_gain = jnp.clip(1.0 + 0.15 * jax.random.normal(key_list[9], (VD,), jnp.float32), 0.25, 1.75)
    merge_up = centred(key_list[10], (4 * VD, MH), (4 * VD) ** -0.5, 0.078125, ((1, 8),))
    merge_up_bias = centred(key_list[11], (MH,), 0.3, 4.0, ((0, 8),), jnp.float32)
    merge_down = centred(key_list[12], (MH, D), MH ** -0.5, 0.125, ((0, 8),))
    merge_down_bias = centred(key_list[13], (D,), 0.3, 4.0, (), jnp.float32)
    input_gain = jnp.clip(1.0 + 0.15 * jax.random.normal(key_list[14], (D,), jnp.float32), 0.25, 1.75)
    kv_weight = centred(key_list[15], (D, 2 * KV_HEADS * HEAD), D ** -0.5, 0.0625, ((1, 8),))
    kv_bias = centred(key_list[16], (2 * KV_HEADS * HEAD,), 0.5, 4.0, ((0, 8),), jnp.float32)
    return {"patches": patches, "image_place": image_place, "slot_map": slot_map, "text": text, "vision_gain": vision_gain, "qkv_weight": qkv_weight, "qkv_bias": qkv_bias, "out_weight": out_weight, "out_bias": out_bias, "merge_gain": merge_gain, "merge_up": merge_up, "merge_up_bias": merge_up_bias, "merge_down": merge_down, "merge_down_bias": merge_down_bias, "input_gain": input_gain, "kv_weight": kv_weight, "kv_bias": kv_bias}


NORM_EPS = 1e-06

def rms_norm(values, gain):
    return values * lax.rsqrt(lax.optimization_barrier(jnp.mean(values * values, axis=-1, keepdims=True)) + NORM_EPS) * gain

def round_trip(values):
    return lax.optimization_barrier(values.astype(jnp.bfloat16)).astype(jnp.float32)

def encode_group(group_patches, group_place, vision_gain, qkv_weight, qkv_bias, out_weight, out_bias, merge_gain, merge_up, merge_up_bias, merge_down, merge_down_bias):
    float_rows = group_patches.astype(jnp.float32)
    normed_rows = round_trip(rms_norm(float_rows, vision_gain))
    projected = jnp.einsum('rd,dtc->trc', normed_rows, qkv_weight.astype(jnp.float32)) + qkv_bias[:, None, :]
    projected = round_trip(projected)
    split_shape = (SHARDS, WIN, VHEADS, VHEAD)
    queries = projected[0].reshape(split_shape)
    key_rows = projected[1].reshape(split_shape)
    value_rows = projected[2].reshape(split_shape)
    scores = jnp.einsum('bqhe,bkhe->bhqk', queries, key_rows) / math.sqrt(VHEAD)
    key_mask = jnp.repeat((group_place >= 0).astype(jnp.float32), 4, axis=1)
    raised = jnp.exp(scores) * key_mask[:, None, None, :]
    probs = round_trip(raised / lax.optimization_barrier(jnp.sum(raised, axis=-1, keepdims=True)))
    head_out = round_trip(jnp.einsum('bhqk,bkhe->bqhe', probs, value_rows)).reshape(VROWS, VD)
    grouped = head_out.reshape(VROWS, HEAD_GROUPS, VD // HEAD_GROUPS)
    weight_groups = out_weight.astype(jnp.float32).reshape(HEAD_GROUPS, VD // HEAD_GROUPS, VD)

    def add_group(group_index, running_sum):
        head_piece = lax.dynamic_index_in_dim(grouped, group_index, 1, keepdims=False)
        weight_piece = lax.dynamic_index_in_dim(weight_groups, group_index, 0, keepdims=False)
        return running_sum + round_trip(jnp.dot(head_piece, weight_piece))
    attended = lax.fori_loop(0, HEAD_GROUPS, add_group, jnp.zeros((VROWS, VD), jnp.float32))
    residual_rows = float_rows + attended + out_bias
    merge_rows = rms_norm(residual_rows, merge_gain).astype(jnp.bfloat16).reshape(SHARDS * UNITS, 4 * VD)
    hidden_rows = jax.nn.gelu(jnp.dot(merge_rows, merge_up, preferred_element_type=jnp.float32) + merge_up_bias, approximate=False).astype(jnp.bfloat16)
    image_rows = jnp.dot(hidden_rows, merge_down, preferred_element_type=jnp.float32) + merge_down_bias
    return image_rows.astype(jnp.bfloat16).reshape(SHARDS, UNITS, D)

def reference(patches, image_place, slot_map, text, vision_gain, qkv_weight, qkv_bias, out_weight, out_bias, merge_gain, merge_up, merge_up_bias, merge_down, merge_down_bias, input_gain, kv_weight, kv_bias):

    def encode_one(pair):
        return encode_group(pair[0], pair[1], vision_gain, qkv_weight, qkv_bias, out_weight, out_bias, merge_gain, merge_up, merge_up_bias, merge_down, merge_down_bias)
    images = lax.map(encode_one, (patches, image_place))
    starts = (jnp.arange(SHARDS, dtype=jnp.int32) * CTX)[:, None]

    def prefill_one(triple):
        shard_text, shard_images, shard_place = triple
        target = jnp.where(shard_place >= 0, starts + shard_place, PROMPT).astype(jnp.int32).reshape(-1)
        prompt = shard_text.at[target].set(shard_images.reshape(-1, D), mode='drop')
        normed = rms_norm(prompt.astype(jnp.float32), input_gain).astype(jnp.bfloat16)
        keyval = (jnp.dot(normed, kv_weight, preferred_element_type=jnp.float32) + kv_bias).astype(jnp.bfloat16)
        return keyval.reshape(SHARDS, CTX, 2, KV_HEADS * HEAD).transpose(2, 0, 1, 3)
    per_shard = lax.map(prefill_one, (text, images.transpose(1, 0, 2, 3), image_place.transpose(1, 0, 2)))
    flat = per_shard.transpose(1, 0, 2, 3, 4).reshape(2, SLOTS, CTX, KV_HEADS * HEAD)
    cache = jnp.zeros((2, SLOTS, CTX, KV_HEADS * HEAD), jnp.bfloat16)
    return cache.at[:, slot_map.reshape(-1)].set(flat)
```

```python
import functools
import math

import jax
import jax.numpy as jnp
from jax import lax
from jax.experimental import pallas as pl
from jax.experimental.pallas import tpu as pltpu
from jax.sharding import PartitionSpec as P

VHEAD = 80
CTX = 32
WIN = 64
JOIN = 4
NORM_EPS = 1e-06
F32 = jnp.float32
BF16 = jnp.bfloat16
VMEM_LIMIT = 48 * 1024 * 1024
NT = (((1,), (1,)), ((), ()))


def call(kernel, outs, args, scratch=(), smem=0, flops=0):
    vmem = pl.BlockSpec(memory_space=pltpu.VMEM)
    scalar = pl.BlockSpec(memory_space=pltpu.SMEM)
    moved = sum(math.prod(a.shape) * a.dtype.itemsize for a in list(args) + list(outs))
    return pl.pallas_call(
        kernel,
        out_shape=outs,
        in_specs=[scalar] * smem + [vmem] * (len(args) - smem),
        out_specs=[vmem] * len(outs),
        scratch_shapes=list(scratch),
        compiler_params=pltpu.CompilerParams(vmem_limit_bytes=VMEM_LIMIT),
        cost_estimate=pl.CostEstimate(flops=flops, bytes_accessed=moved, transcendentals=0),
    )(*args)


def struct(shape, dtype):
    return jax.ShapeDtypeStruct(shape, dtype)


def shifted(x, axis, count, k):
    return lax.ppermute(x, axis, [(i, (i + k) % count) for i in range(count)])


def chunk_of(section, z, n_z):
    return section * (n_z // JOIN) + z // JOIN


def front_kernel(n_z, block, place, x_ref, gain_ref, w_ref, b_ref, wo_ref, ob_ref,
                 keep_ref, send_ref, base_ref, hf):
    c, z, s = lax.axis_index("section"), lax.axis_index("mp"), lax.axis_index("seq")
    rows, width = x_ref.shape
    head_width = hf.shape[1]
    units = place.shape[2]
    tile = 256
    per_tile = tile // WIN

    def one(t, carry):
        at = pl.ds(pl.multiple_of(t * tile, tile), tile)
        x = x_ref[at, :].astype(F32)
        scale = lax.rsqrt(jnp.mean(x * x, axis=-1, keepdims=True) + NORM_EPS)
        y = (x * scale * gain_ref[...]).astype(BF16)
        parts = []
        for i in range(3):
            w = w_ref[i * head_width:(i + 1) * head_width, :]
            part = lax.dot_general(y, w, NT, preferred_element_type=F32)
            parts.append((part + b_ref[i:i + 1, :]).astype(BF16))
        q, k, v = parts
        key = lax.broadcasted_iota(jnp.int32, (tile, tile), 1)
        row = lax.broadcasted_iota(jnp.int32, (tile, tile), 0)
        same = key // WIN == row // WIN
        end = jnp.zeros((tile, tile), jnp.int32)
        for j in range(per_tile):
            count = jnp.int32(0)
            for u in range(units):
                count += (place[s, t * per_tile + j, u] >= 0).astype(jnp.int32)
            end = jnp.where(key // WIN == j, j * WIN + count * JOIN, end)
        live = same & (key < end)
        lane = lax.broadcasted_iota(jnp.int32, (1, head_width), 1)
        total = jnp.zeros((tile, head_width), F32)
        for h in range(head_width // VHEAD):
            mine = lane // VHEAD == h
            qh = jnp.where(mine, q, jnp.zeros_like(q))
            scores = lax.dot_general(qh, k, NT, preferred_element_type=F32) * (1.0 / math.sqrt(VHEAD))
            raised = jnp.where(live, jnp.exp(scores), 0.0)
            probs = (raised / jnp.sum(raised, axis=-1, keepdims=True)).astype(BF16)
            out = jnp.dot(probs, v, preferred_element_type=F32)
            total = jnp.where(mine, out, total)
        hf[at, :] = total.astype(BF16)
        return carry

    if rows == tile:
        one(0, 0)
    else:
        lax.fori_loop(0, rows // tile, one, 0)

    def picked(section, zz, count):
        i = lax.broadcasted_iota(jnp.int32, (count, rows), 0)
        device = zz + i // block
        first = JOIN * block * chunk_of(section, device, n_z) + device % JOIN
        source = first + JOIN * (i % block)
        return (lax.broadcasted_iota(jnp.int32, (count, rows), 1) == source).astype(BF16)

    wo = wo_ref[...]
    heads = hf[...]
    for section, out in ((1 - c, send_ref), (c, keep_ref)):
        order = picked(section, 0, rows // 2)
        chosen = jnp.dot(order, heads, preferred_element_type=F32).astype(BF16)
        out[...] = jnp.dot(chosen, wo, preferred_element_type=F32).astype(BF16)
    own = jnp.dot(picked(c, z, block), x_ref[...], preferred_element_type=F32)
    base_ref[...] = own + ob_ref[...]


def pair_rows_kernel(n_z, block, keep_ref, got_ref, *outs):
    z = lax.axis_index("mp")
    for k in range(n_z):
        at = pl.ds(pl.multiple_of(lax.rem(z + k, n_z) * block, block), block)
        total = keep_ref[at, :].astype(F32) + got_ref[at, :].astype(F32)
        outs[k][...] = total.astype(outs[k].dtype)


def resid_kernel(base_ref, gain_ref, own_ref, *refs):
    out_ref = refs[-1]
    total = own_ref[...]
    for r in refs[:-1]:
        total += r[...].astype(F32)
    x = base_ref[...] + total
    scale = lax.rsqrt(jnp.mean(x * x, axis=-1, keepdims=True) + NORM_EPS)
    out_ref[...] = (x * scale * gain_ref[...]).astype(BF16)


def merge_kernel(n_z, block, up_ref, ub_ref, down_ref, *refs):
    c, z = lax.axis_index("section"), lax.axis_index("mp")
    pieces, (keep_ref, send_ref, xs) = refs[:2 * n_z], refs[2 * n_z:]
    width = xs.shape[2]
    for side in range(2):
        section = c if side == 0 else 1 - c
        for k in range(n_z):
            zz = lax.rem(z - k + n_z, n_z)
            chunk = chunk_of(section, zz, n_z)
            at = pl.ds(pl.multiple_of(chunk * block, block), block)
            xs[lax.rem(zz, JOIN), at, :] = pieces[side * n_z + k][...]
    acc = ub_ref[...]
    for q in range(JOIN):
        acc = acc + lax.dot_general(
            xs[q], up_ref[:, q * width:(q + 1) * width], NT, preferred_element_type=F32)
    hidden = (0.5 * acc * (1.0 + lax.erf(acc * (1.0 / math.sqrt(2.0))))).astype(BF16)
    half = keep_ref.shape[1]
    for section, out in ((1 - c, send_ref), (c, keep_ref)):
        at = pl.ds(pl.multiple_of(section * half, half), half)
        out[...] = jnp.dot(hidden, down_ref[:, at], preferred_element_type=F32).astype(BF16)


def pair_columns_kernel(n_z, block, keep_ref, got_ref, *outs):
    z = lax.axis_index("mp")
    for k in range(n_z):
        at = pl.ds(pl.multiple_of(lax.rem(z + k, n_z) * block, block), block)
        total = keep_ref[:, at].astype(F32) + got_ref[:, at].astype(F32)
        outs[k][...] = total.astype(outs[k].dtype)


def image_kernel(n_z, bias_ref, own_ref, *refs):
    out_ref = refs[-1]
    block = out_ref.shape[1]
    d = lax.axis_index("section") * n_z + lax.axis_index("mp")
    total = own_ref[...]
    for r in refs[:-1]:
        total += r[...].astype(F32)
    at = pl.ds(pl.multiple_of(d * block, block), block)
    out_ref[...] = (total + bias_ref[:, at]).astype(BF16)


def image_keyval_kernel(n_z, gain_ref, w_ref, b_ref, *refs):
    c, z = lax.axis_index("section"), lax.axis_index("mp")
    pieces, out_ref = refs[:-1], refs[-1]
    rows, block = pieces[0].shape
    acc = jnp.zeros(out_ref.shape, F32)
    squares = jnp.zeros((rows, 1), F32)
    for side in range(2):
        section = c if side == 0 else 1 - c
        for k in range(n_z):
            d = section * n_z + lax.rem(z - k + n_z, n_z)
            at = pl.ds(pl.multiple_of(d * block, block), block)
            x = pieces[side * n_z + k][...].astype(F32)
            squares += jnp.sum(x * x, axis=-1, keepdims=True)
            acc += jnp.dot((x * gain_ref[:, at]).astype(BF16), w_ref[at, :], preferred_element_type=F32)
    scale = lax.rsqrt(squares * (1.0 / w_ref.shape[0]) + NORM_EPS)
    out_ref[...] = (acc * scale + b_ref[...]).astype(BF16)


def text_norm_kernel(x_ref, gain_ref, out_ref):
    x = x_ref[...].astype(F32)
    scale = lax.rsqrt(jnp.mean(x * x, axis=-1, keepdims=True) + NORM_EPS)
    out_ref[...] = (x * scale * gain_ref[...]).astype(BF16)


def text_keyval_kernel(n_z, w_ref, b_ref, *refs):
    c, z = lax.axis_index("section"), lax.axis_index("mp")
    pieces, out_ref = refs[:-1], refs[-1]
    block = pieces[0].shape[0]
    x = jnp.concatenate([p[...] for p in pieces], axis=0)
    acc = jnp.dot(x, w_ref[...], preferred_element_type=F32) + b_ref[...]
    for side in range(2):
        section = c if side == 0 else 1 - c
        for k in range(n_z):
            d = section * n_z + lax.rem(z - k + n_z, n_z)
            at = pl.ds(pl.multiple_of(d * block, block), block)
            i = side * n_z + k
            out_ref[at, :] = acc[i * block:(i + 1) * block].astype(BF16)


def place_kernel(n_s, slot_map, place_ref, *refs):
    s = lax.axis_index("seq")
    texts, images, (out_ref, held) = refs[:n_s], refs[n_s:2 * n_s], refs[2 * n_s:]
    units = place_ref.shape[2]
    for k in range(n_s):
        held[lax.rem(s - k + n_s, n_s)] = images[k][...]
    position = lax.broadcasted_iota(jnp.int32, (CTX, units), 0)
    for k in range(n_s):
        j = lax.rem(s - k + n_s, n_s)

        def one(i, carry):
            slot = slot_map[j, i] - s * n_s

            @pl.when((slot >= 0) & (slot < n_s))
            def _():
                chosen = position == place_ref[i, pl.ds(j, 1), :]
                covered = jnp.sum(chosen.astype(F32), axis=1, keepdims=True) > 0.5
                rows = held[i, pl.ds(pl.multiple_of(j * units, units), units), :]
                image = jnp.dot(chosen.astype(BF16), rows, preferred_element_type=F32)
                text = texts[k][pl.ds(pl.multiple_of(i * CTX, CTX), CTX), :]
                out_ref[slot] = jnp.where(covered, image, text.astype(F32)).astype(BF16)

            return carry

        lax.fori_loop(0, n_s, one, 0)


def shards(
    patches,
    image_place,
    slot_map,
    text,
    vision_gain,
    qkv_weight,
    qkv_bias,
    out_weight,
    out_bias,
    merge_gain,
    merge_up,
    merge_up_bias,
    merge_down,
    merge_down_bias,
    input_gain,
    kv_weight,
    kv_bias,
):
    n_z, n_s = lax.axis_size("mp"), lax.axis_size("seq")
    n_d = lax.axis_size("section") * n_z
    x = patches[0]
    rows, width = x.shape
    units = rows // JOIN
    block = rows // n_d
    head_width = out_weight.shape[0]
    hidden = merge_up.shape[1]
    model = merge_down.shape[1]
    columns = model // n_d
    kv_width = kv_weight.shape[1]

    def flat(v):
        return v.reshape(1, -1)

    def swap(v):
        return lax.ppermute(v, "section", [(0, 1), (1, 0)])

    def spread(own):
        here = [own] + [shifted(own, "mp", n_z, k) for k in range(1, n_z)]
        return here + [swap(v) for v in here]

    text_own, = call(text_norm_kernel, [struct(text.shape[1:], BF16)], [text[0], flat(input_gain)])
    text_pieces = spread(text_own)
    prompt = n_d * text.shape[1]
    text_keyval, = call(
        functools.partial(text_keyval_kernel, n_z),
        [struct((prompt, kv_width), BF16)],
        [kv_weight, flat(kv_bias)] + text_pieces,
        flops=2 * prompt * model * kv_width,
    )
    texts = [text_keyval] + [shifted(text_keyval, "seq", n_s, k) for k in range(1, n_s)]

    w = qkv_weight.transpose(1, 2, 0).reshape(3 * head_width, width)
    keep, send, base = call(
        functools.partial(front_kernel, n_z, block),
        [struct((rows // 2, width), BF16)] * 2 + [struct((block, width), F32)],
        [image_place, x, flat(vision_gain), w, qkv_bias, out_weight, flat(out_bias)],
        [pltpu.VMEM((rows, head_width), BF16)],
        smem=1,
        flops=2 * rows * width * 4 * head_width,
    )
    got = swap(send)
    parts = call(
        functools.partial(pair_rows_kernel, n_z, block),
        [struct((block, width), F32)] + [struct((block, width), BF16)] * (n_z - 1),
        [keep, got],
    )
    sums = [parts[0]] + [shifted(parts[k], "mp", n_z, k) for k in range(1, n_z)]
    merged, = call(resid_kernel, [struct((block, width), BF16)], [base, flat(merge_gain)] + sums)
    pieces = spread(merged)

    keep, send = call(
        functools.partial(merge_kernel, n_z, block),
        [struct((units, model // 2), BF16)] * 2,
        [merge_up.T, flat(merge_up_bias), merge_down] + pieces,
        [pltpu.VMEM((JOIN, units, width), BF16)],
        flops=2 * units * hidden * (JOIN * width + model),
    )
    got = swap(send)
    parts = call(
        functools.partial(pair_columns_kernel, n_z, columns),
        [struct((units, columns), F32)] + [struct((units, columns), BF16)] * (n_z - 1),
        [keep, got],
    )
    sums = [parts[0]] + [shifted(parts[k], "mp", n_z, k) for k in range(1, n_z)]
    image, = call(
        functools.partial(image_kernel, n_z), [struct((units, columns), BF16)], [flat(merge_down_bias)] + sums)
    image_pieces = spread(image)

    image_keyval, = call(
        functools.partial(image_keyval_kernel, n_z),
        [struct((units, kv_width), BF16)],
        [flat(input_gain), kv_weight, flat(kv_bias)] + image_pieces,
        flops=2 * units * model * kv_width,
    )
    images = [image_keyval] + [shifted(image_keyval, "seq", n_s, k) for k in range(1, n_s)]
    cache, = call(
        functools.partial(place_kernel, n_s),
        [struct((n_s, CTX, kv_width), BF16)],
        [slot_map, image_place] + texts + images,
        [pltpu.VMEM((n_s, units, kv_width), BF16)],
        smem=1,
    )
    return cache[None]


def solution(mesh):
    placed = (
        P("seq", None, None),
        P(),
        P(),
        P("seq", ("section", "mp"), None),
        P(),
        P(None, None, ("section", "mp")),
        P(None, ("section", "mp")),
        P(("section", "mp"), None),
        P(),
        P(),
        P(None, ("section", "mp")),
        P(("section", "mp")),
        P(("section", "mp"), None),
        P(),
        P(),
        P(None, ("section", "mp")),
        P(("section", "mp")),
    )
    return jax.shard_map(
        shards,
        mesh=mesh,
        in_specs=placed,
        out_specs=P("section", "seq", None, "mp"),
        check_vma=False,
    )
```

```python
import functools
import math

import jax
import jax.numpy as jnp
from jax import lax
from jax.experimental import pallas as pl
from jax.experimental.pallas import tpu as pltpu
from jax.sharding import PartitionSpec as P

VHEAD = 80
CTX = 32
WIN = 64
JOIN = 4
NORM_EPS = 1e-06
F32 = jnp.float32
BF16 = jnp.bfloat16
MIB = 1024 * 1024
NT = (((1,), (1,)), ((), ()))


def call(kernel, outs, args, after=(), scratch=(), smem=0, raw=False, flops=0, grant=8):
    space = pl.BlockSpec(memory_space=pltpu.HBM if raw else pltpu.VMEM)
    scalar = pl.BlockSpec(memory_space=pltpu.SMEM)
    unread = pl.BlockSpec(memory_space=pl.ANY)
    moved = sum(math.prod(a.shape) * a.dtype.itemsize for a in list(args) + list(outs))
    count = len(after)
    if raw:
        args = [pltpu.with_memory_space_constraint(a, pltpu.HBM) for a in args]

    def body(*refs):
        kernel(*refs[count:])

    return pl.pallas_call(
        body,
        out_shape=outs,
        in_specs=[unread] * count + [scalar] * smem + [space] * (len(args) - smem),
        out_specs=[pl.BlockSpec(memory_space=pltpu.VMEM)] * len(outs),
        scratch_shapes=list(scratch),
        compiler_params=pltpu.CompilerParams(vmem_limit_bytes=grant * MIB),
        cost_estimate=pl.CostEstimate(flops=flops, bytes_accessed=moved, transcendentals=0),
    )(*after, *args)


def struct(shape, dtype):
    return jax.ShapeDtypeStruct(shape, dtype)


def shifted(x, axis, count, k):
    return lax.ppermute(x, axis, [(i, (i + k) % count) for i in range(count)])


def chunk_of(section, z, n_z):
    return section * (n_z // JOIN) + z // JOIN


def front_kernel(n_z, block, kept, place_hbm, x_hbm, gain_hbm, w_hbm, b_hbm, wo_hbm, ob_hbm, *refs):
    later, refs = refs[:kept], refs[kept:]
    (keep_ref, send_ref, base_ref), held, refs = refs[:3], refs[3:3 + kept], refs[3 + kept:]
    hf, place, x_ref, gain_ref, w_ref, b_ref, wo_ref, ob_ref, sems = refs
    brought = (
        (x_hbm, x_ref), (gain_hbm, gain_ref), (w_hbm, w_ref), (b_hbm, b_ref),
        (place_hbm, place), (wo_hbm, wo_ref), (ob_hbm, ob_ref), *zip(later, held),
    )
    copies = [pltpu.make_async_copy(a, b, sems.at[i]) for i, (a, b) in enumerate(brought)]
    for copy in copies:
        copy.start()
    c, z, s = lax.axis_index("section"), lax.axis_index("mp"), lax.axis_index("seq")
    rows, width = x_ref.shape
    head_width = hf.shape[1]
    units = place.shape[2]
    tile = 256
    per_tile = tile // WIN
    for copy in copies[:5]:
        copy.wait()

    def one(t, carry):
        at = pl.ds(pl.multiple_of(t * tile, tile), tile)
        x = x_ref[at, :].astype(F32)
        scale = lax.rsqrt(jnp.mean(x * x, axis=-1, keepdims=True) + NORM_EPS)
        y = (x * scale * gain_ref[...][None, :]).astype(BF16)
        parts = []
        for i in range(3):
            w = w_ref[i * head_width:(i + 1) * head_width, :]
            part = lax.dot_general(y, w, NT, preferred_element_type=F32)
            parts.append((part + b_ref[i:i + 1, :]).astype(BF16))
        q, k, v = parts
        key = lax.broadcasted_iota(jnp.int32, (tile, tile), 1)
        row = lax.broadcasted_iota(jnp.int32, (tile, tile), 0)
        same = key // WIN == row // WIN
        end = jnp.zeros((tile, tile), jnp.int32)
        for j in range(per_tile):
            count = jnp.int32(0)
            for u in range(units):
                count += (place[s, t * per_tile + j, u] >= 0).astype(jnp.int32)
            end = jnp.where(key // WIN == j, j * WIN + count * JOIN, end)
        live = same & (key < end)
        lane = lax.broadcasted_iota(jnp.int32, (1, head_width), 1)
        total = jnp.zeros((tile, head_width), F32)
        for h in range(head_width // VHEAD):
            mine = lane // VHEAD == h
            qh = jnp.where(mine, q, jnp.zeros_like(q))
            scores = lax.dot_general(qh, k, NT, preferred_element_type=F32) * (1.0 / math.sqrt(VHEAD))
            raised = jnp.where(live, jnp.exp(scores), 0.0)
            probs = (raised / jnp.sum(raised, axis=-1, keepdims=True)).astype(BF16)
            out = jnp.dot(probs, v, preferred_element_type=F32)
            total = jnp.where(mine, out, total)
        hf[at, :] = total.astype(BF16)
        return carry

    if rows == tile:
        one(0, 0)
    else:
        lax.fori_loop(0, rows // tile, one, 0)

    def picked(section, zz, count):
        i = lax.broadcasted_iota(jnp.int32, (count, rows), 0)
        device = zz + i // block
        first = JOIN * block * chunk_of(section, device, n_z) + device % JOIN
        source = first + JOIN * (i % block)
        return (lax.broadcasted_iota(jnp.int32, (count, rows), 1) == source).astype(BF16)

    copies[5].wait()
    copies[6].wait()
    wo = wo_ref[...]
    heads = hf[...]
    for section, out in ((1 - c, send_ref), (c, keep_ref)):
        order = picked(section, 0, rows // 2)
        chosen = jnp.dot(order, heads, preferred_element_type=F32).astype(BF16)
        out[...] = jnp.dot(chosen, wo, preferred_element_type=F32).astype(BF16)
    own = jnp.dot(picked(c, z, block), x_ref[...], preferred_element_type=F32)
    base_ref[...] = own + ob_ref[...][None, :]
    for copy in copies[7:]:
        copy.wait()


def pair_rows_kernel(n_z, block, keep_ref, got_ref, *outs):
    z = lax.axis_index("mp")
    for k in range(n_z):
        at = pl.ds(pl.multiple_of(lax.rem(z + k, n_z) * block, block), block)
        total = keep_ref[at, :].astype(F32) + got_ref[at, :].astype(F32)
        outs[k][...] = total.astype(outs[k].dtype)


def resid_kernel(base_ref, gain_ref, own_ref, *refs):
    out_ref = refs[-1]
    total = own_ref[...]
    for r in refs[:-1]:
        total += r[...].astype(F32)
    x = base_ref[...] + total
    scale = lax.rsqrt(jnp.mean(x * x, axis=-1, keepdims=True) + NORM_EPS)
    out_ref[...] = (x * scale * gain_ref[...][None, :]).astype(BF16)


def hidden_kernel(n_z, block, up_ref, ub_ref, *refs):
    c, z = lax.axis_index("section"), lax.axis_index("mp")
    pieces, (out_ref, xs) = refs[:2 * n_z], refs[2 * n_z:]
    width = xs.shape[2]
    for side in range(2):
        section = c if side == 0 else 1 - c
        for k in range(n_z):
            zz = lax.rem(z - k + n_z, n_z)
            chunk = chunk_of(section, zz, n_z)
            at = pl.ds(pl.multiple_of(chunk * block, block), block)
            xs[lax.rem(zz, JOIN), at, :] = pieces[side * n_z + k][...]
    acc = ub_ref[...][None, :]
    for q in range(JOIN):
        acc = acc + lax.dot_general(
            xs[q], up_ref[:, q * width:(q + 1) * width], NT, preferred_element_type=F32)
    out_ref[...] = (0.5 * acc * (1.0 + lax.erf(acc * (1.0 / math.sqrt(2.0))))).astype(BF16)


def down_kernel(other, hidden_ref, down_ref, out_ref):
    c = lax.axis_index("section")
    half = out_ref.shape[1]
    at = pl.ds(pl.multiple_of((1 - c if other else c) * half, half), half)
    out_ref[...] = jnp.dot(hidden_ref[...], down_ref[:, at], preferred_element_type=F32).astype(BF16)


def pair_columns_kernel(n_z, block, keep_ref, got_ref, *outs):
    z = lax.axis_index("mp")
    for k in range(n_z):
        at = pl.ds(pl.multiple_of(lax.rem(z + k, n_z) * block, block), block)
        total = keep_ref[:, at].astype(F32) + got_ref[:, at].astype(F32)
        outs[k][...] = total.astype(outs[k].dtype)


def image_kernel(n_z, bias_ref, own_ref, *refs):
    out_ref = refs[-1]
    block = out_ref.shape[1]
    d = lax.axis_index("section") * n_z + lax.axis_index("mp")
    total = own_ref[...]
    for r in refs[:-1]:
        total += r[...].astype(F32)
    at = pl.ds(pl.multiple_of(d * block, block), block)
    out_ref[...] = (total + bias_ref[at][None, :]).astype(BF16)


def image_keyval_kernel(n_z, text_ref, gain_ref, w_ref, b_ref, *refs):
    c, z = lax.axis_index("section"), lax.axis_index("mp")
    pieces, out_ref = refs[:-1], refs[-1]
    rows, block = pieces[0].shape
    prompt = text_ref.shape[0]
    out_ref[:prompt, :] = text_ref[...]
    acc = jnp.zeros((rows, out_ref.shape[1]), F32)
    squares = jnp.zeros((rows, 1), F32)
    for side in range(2):
        section = c if side == 0 else 1 - c
        for k in range(n_z):
            d = section * n_z + lax.rem(z - k + n_z, n_z)
            at = pl.ds(pl.multiple_of(d * block, block), block)
            x = pieces[side * n_z + k][...].astype(F32)
            squares += jnp.sum(x * x, axis=-1, keepdims=True)
            acc += jnp.dot((x * gain_ref[at][None, :]).astype(BF16), w_ref[at, :], preferred_element_type=F32)
    scale = lax.rsqrt(squares * (1.0 / w_ref.shape[0]) + NORM_EPS)
    out_ref[prompt:, :] = (acc * scale + b_ref[...][None, :]).astype(BF16)


def relay_kernel(in_ref, out_ref):
    out_ref[...] = in_ref[...]


def text_keyval_kernel(n_z, gain_ref, w_ref, b_ref, *refs):
    c, z = lax.axis_index("section"), lax.axis_index("mp")
    pieces, out_ref = refs[:-1], refs[-1]
    block, model = pieces[0].shape
    acc = jnp.zeros(out_ref.shape, F32)
    squares = jnp.zeros((out_ref.shape[0], 1), F32)
    step = 1024
    for first in range(0, model, step):
        x = jnp.concatenate([p[:, first:first + step] for p in pieces], axis=0).astype(F32)
        squares += jnp.sum(x * x, axis=-1, keepdims=True)
        y = (x * gain_ref[first:first + step][None, :]).astype(BF16)
        acc += jnp.dot(y, w_ref[first:first + step, :], preferred_element_type=F32)
    scale = lax.rsqrt(squares * (1.0 / model) + NORM_EPS)
    acc = acc * scale + b_ref[...][None, :]
    for side in range(2):
        section = c if side == 0 else 1 - c
        for k in range(n_z):
            d = section * n_z + lax.rem(z - k + n_z, n_z)
            at = pl.ds(pl.multiple_of(d * block, block), block)
            i = side * n_z + k
            out_ref[at, :] = acc[i * block:(i + 1) * block].astype(BF16)


def place_kernel(n_s, slot_map, place_ref, *refs):
    s = lax.axis_index("seq")
    keyvals, (out_ref, held) = refs[:n_s], refs[n_s:]
    units = place_ref.shape[2]
    prompt = n_s * CTX
    for k in range(n_s):
        held[lax.rem(s - k + n_s, n_s)] = keyvals[k][prompt:, :]
    position = lax.broadcasted_iota(jnp.int32, (CTX, units), 0)
    for k in range(n_s):
        j = lax.rem(s - k + n_s, n_s)

        def one(i, carry):
            slot = slot_map[j, i] - s * n_s

            @pl.when((slot >= 0) & (slot < n_s))
            def _():
                chosen = position == place_ref[i, pl.ds(j, 1), :]
                covered = jnp.sum(chosen.astype(F32), axis=1, keepdims=True) > 0.5
                rows = held[i, pl.ds(pl.multiple_of(j * units, units), units), :]
                image = jnp.dot(chosen.astype(BF16), rows, preferred_element_type=F32)
                text = keyvals[k][pl.ds(pl.multiple_of(i * CTX, CTX), CTX), :]
                out_ref[slot] = jnp.where(covered, image, text.astype(F32)).astype(BF16)

            return carry

        lax.fori_loop(0, n_s, one, 0)


def shards(
    patches,
    image_place,
    slot_map,
    text,
    vision_gain,
    qkv_weight,
    qkv_bias,
    out_weight,
    out_bias,
    merge_gain,
    merge_up,
    merge_up_bias,
    merge_down,
    merge_down_bias,
    input_gain,
    kv_weight,
    kv_bias,
):
    n_z, n_s = lax.axis_size("mp"), lax.axis_size("seq")
    n_d = lax.axis_size("section") * n_z
    x = patches[0]
    rows, width = x.shape
    units = rows // JOIN
    block = rows // n_d
    head_width = out_weight.shape[0]
    model = merge_down.shape[1]
    columns = model // n_d
    kv_width = kv_weight.shape[1]

    def swap(v):
        return lax.ppermute(v, "section", [(0, 1), (1, 0)])

    def spread(own):
        here = [own] + [shifted(own, "mp", n_z, k) for k in range(1, n_z)]
        return here + [swap(v) for v in here]

    text_own = text[0]
    text_at = {k: shifted(text_own, "mp", n_z, k) for k in range(1, n_z)}

    w = qkv_weight.transpose(1, 2, 0).reshape(3 * head_width, width)
    later = [merge_gain, merge_up.T, merge_up_bias, merge_down_bias, input_gain, kv_bias]
    keep, send, base, gain, up, up_bias, down_bias, text_gain, bias = call(
        functools.partial(front_kernel, n_z, block, len(later)),
        [struct((rows // 2, width), BF16)] * 2 + [struct((block, width), F32)]
        + [struct(v.shape, v.dtype) for v in later],
        [image_place, x, vision_gain, w, qkv_bias, out_weight, out_bias] + later,
        scratch=[
            pltpu.VMEM((rows, head_width), BF16), pltpu.SMEM(image_place.shape, jnp.int32),
            pltpu.VMEM(x.shape, BF16), pltpu.VMEM(vision_gain.shape, F32), pltpu.VMEM(w.shape, BF16),
            pltpu.VMEM(qkv_bias.shape, F32), pltpu.VMEM(out_weight.shape, BF16), pltpu.VMEM(out_bias.shape, F32),
            pltpu.SemaphoreType.DMA((7 + len(later),)),
        ],
        raw=True,
        grant=24,
        flops=2 * rows * width * 4 * head_width,
    )
    got = swap(send)
    parts = call(
        functools.partial(pair_rows_kernel, n_z, block),
        [struct((block, width), F32)] + [struct((block, width), BF16)] * (n_z - 1),
        [keep, got],
    )
    sums = [parts[0]] + [shifted(parts[k], "mp", n_z, k) for k in range(1, n_z)]
    merged, = call(
        resid_kernel, [struct((block, width), BF16)], [base, gain] + sums, after=[text_at[1]])
    pieces = spread(merged)

    hidden, = call(
        functools.partial(hidden_kernel, n_z, block),
        [struct((units, merge_up.shape[1]), BF16)],
        [up, up_bias] + pieces,
        scratch=[pltpu.VMEM((JOIN, units, width), BF16)],
        flops=2 * units * merge_up.size,
    )
    send, keep = (
        call(
            functools.partial(down_kernel, other),
            [struct((units, model // 2), BF16)],
            [hidden, merge_down],
            flops=units * merge_down.size,
            grant=16,
        )[0]
        for other in (True, False)
    )
    got = swap(send)
    parts = call(
        functools.partial(pair_columns_kernel, n_z, columns),
        [struct((units, columns), F32)] + [struct((units, columns), BF16)] * (n_z - 1),
        [keep, got],
        after=[text_at[n_z - 1]],
    )
    sums = [parts[0]] + [shifted(parts[k], "mp", n_z, k) for k in range(1, n_z)]
    image, = call(
        functools.partial(image_kernel, n_z), [struct((units, columns), BF16)], [down_bias] + sums)
    image_pieces = spread(image)

    for k in range(2, n_z - 1):
        text_at[k] = call(relay_kernel, [struct(text_own.shape, BF16)], [text_at[k]], after=[image])[0]
    text_here = [text_own] + [text_at[k] for k in range(1, n_z)]
    prompt = n_d * text.shape[1]
    text_keyval, = call(
        functools.partial(text_keyval_kernel, n_z),
        [struct((prompt, kv_width), BF16)],
        [text_gain, kv_weight, bias] + text_here + [swap(v) for v in text_here],
        flops=2 * prompt * model * kv_width,
        grant=16,
    )

    keyval, = call(
        functools.partial(image_keyval_kernel, n_z),
        [struct((prompt + units, kv_width), BF16)],
        [text_keyval, text_gain, kv_weight, bias] + image_pieces,
        flops=2 * units * model * kv_width,
        grant=16,
    )
    keyvals = [keyval] + [shifted(keyval, "seq", n_s, k) for k in range(1, n_s)]
    cache, = call(
        functools.partial(place_kernel, n_s),
        [struct((n_s, CTX, kv_width), BF16)],
        [slot_map, image_place] + keyvals,
        scratch=[pltpu.VMEM((n_s, units, kv_width), BF16)],
        smem=1,
        grant=16,
    )
    return cache[None]


def solution(mesh):
    placed = (
        P("seq", None, None),
        P(),
        P(),
        P("seq", ("section", "mp"), None),
        P(),
        P(None, None, ("section", "mp")),
        P(None, ("section", "mp")),
        P(("section", "mp"), None),
        P(),
        P(),
        P(None, ("section", "mp")),
        P(("section", "mp")),
        P(("section", "mp"), None),
        P(),
        P(),
        P(None, ("section", "mp")),
        P(("section", "mp")),
    )
    return jax.shard_map(
        shards,
        mesh=mesh,
        in_specs=placed,
        out_specs=P("section", "seq", None, "mp"),
        check_vma=False,
    )
```

```python
import functools
import math

import jax
import jax.numpy as jnp
from jax import lax
from jax.experimental import pallas as pl
from jax.experimental.pallas import tpu as pltpu
from jax.sharding import PartitionSpec as P

VHEAD = 80
CTX = 32
WIN = 64
JOIN = 4
NORM_EPS = 1e-06
F32 = jnp.float32
BF16 = jnp.bfloat16
MIB = 1024 * 1024
NT = (((1,), (1,)), ((), ()))


def call(kernel, outs, args, after=(), scratch=(), smem=0, raw=False, flops=0, grant=8):
    space = pl.BlockSpec(memory_space=pltpu.HBM if raw else pltpu.VMEM)
    scalar = pl.BlockSpec(memory_space=pltpu.SMEM)
    unread = pl.BlockSpec(memory_space=pl.ANY)
    moved = sum(math.prod(a.shape) * a.dtype.itemsize for a in list(args) + list(outs))
    count = len(after)
    if raw:
        args = [pltpu.with_memory_space_constraint(a, pltpu.HBM) for a in args]

    def body(*refs):
        kernel(*refs[count:])

    return pl.pallas_call(
        body,
        out_shape=outs,
        in_specs=[unread] * count + [scalar] * smem + [space] * (len(args) - smem),
        out_specs=[pl.BlockSpec(memory_space=pltpu.VMEM)] * len(outs),
        scratch_shapes=list(scratch),
        compiler_params=pltpu.CompilerParams(vmem_limit_bytes=grant * MIB),
        cost_estimate=pl.CostEstimate(flops=flops, bytes_accessed=moved, transcendentals=0),
    )(*after, *args)


def struct(shape, dtype):
    return jax.ShapeDtypeStruct(shape, dtype)


def shifted(x, axis, count, k):
    return lax.ppermute(x, axis, [(i, (i + k) % count) for i in range(count)])


def chunk_of(section, z, n_z):
    return section * (n_z // JOIN) + z // JOIN


def front_kernel(n_z, block, kept, place_hbm, x_hbm, gain_hbm, w_hbm, b_hbm, wo_hbm, ob_hbm, *refs):
    later, refs = refs[:kept], refs[kept:]
    (keep_ref, send_ref, base_ref), held, refs = refs[:3], refs[3:3 + kept], refs[3 + kept:]
    hf, place, x_ref, gain_ref, w_ref, b_ref, wo_ref, ob_ref, sems = refs
    brought = (
        (x_hbm, x_ref), (gain_hbm, gain_ref), (w_hbm, w_ref), (b_hbm, b_ref),
        (place_hbm, place), (wo_hbm, wo_ref), (ob_hbm, ob_ref), *zip(later, held),
    )
    copies = [pltpu.make_async_copy(a, b, sems.at[i]) for i, (a, b) in enumerate(brought)]
    for copy in copies:
        copy.start()
    c, z, s = lax.axis_index("section"), lax.axis_index("mp"), lax.axis_index("seq")
    rows, width = x_ref.shape
    head_width = hf.shape[1]
    units = place.shape[2]
    tile = 256
    per_tile = tile // WIN
    for copy in copies[:5]:
        copy.wait()

    def one(t, carry):
        at = pl.ds(pl.multiple_of(t * tile, tile), tile)
        x = x_ref[at, :].astype(F32)
        scale = lax.rsqrt(jnp.mean(x * x, axis=-1, keepdims=True) + NORM_EPS)
        y = (x * scale * gain_ref[...][None, :]).astype(BF16)
        parts = []
        for i in range(3):
            w = w_ref[i * head_width:(i + 1) * head_width, :]
            part = lax.dot_general(y, w, NT, preferred_element_type=F32)
            parts.append((part + b_ref[i:i + 1, :]).astype(BF16))
        q, k, v = parts
        key = lax.broadcasted_iota(jnp.int32, (tile, tile), 1)
        row = lax.broadcasted_iota(jnp.int32, (tile, tile), 0)
        same = key // WIN == row // WIN
        end = jnp.zeros((tile, tile), jnp.int32)
        for j in range(per_tile):
            count = jnp.int32(0)
            for u in range(units):
                count += (place[s, t * per_tile + j, u] >= 0).astype(jnp.int32)
            end = jnp.where(key // WIN == j, j * WIN + count * JOIN, end)
        live = same & (key < end)
        lane = lax.broadcasted_iota(jnp.int32, (1, head_width), 1)
        total = jnp.zeros((tile, head_width), F32)
        for h in range(head_width // VHEAD):
            mine = lane // VHEAD == h
            qh = jnp.where(mine, q, jnp.zeros_like(q))
            scores = lax.dot_general(qh, k, NT, preferred_element_type=F32) * (1.0 / math.sqrt(VHEAD))
            raised = jnp.where(live, jnp.exp(scores), 0.0)
            probs = (raised / jnp.sum(raised, axis=-1, keepdims=True)).astype(BF16)
            out = jnp.dot(probs, v, preferred_element_type=F32)
            total = jnp.where(mine, out, total)
        hf[at, :] = total.astype(BF16)
        return carry

    if rows == tile:
        one(0, 0)
    else:
        lax.fori_loop(0, rows // tile, one, 0)

    def picked(section, zz, count):
        i = lax.broadcasted_iota(jnp.int32, (count, rows), 0)
        device = zz + i // block
        first = JOIN * block * chunk_of(section, device, n_z) + device % JOIN
        source = first + JOIN * (i % block)
        return (lax.broadcasted_iota(jnp.int32, (count, rows), 1) == source).astype(BF16)

    copies[5].wait()
    copies[6].wait()
    wo = wo_ref[...]
    heads = hf[...]
    for section, out in ((1 - c, send_ref), (c, keep_ref)):
        order = picked(section, 0, rows // 2)
        chosen = jnp.dot(order, heads, preferred_element_type=F32).astype(BF16)
        out[...] = jnp.dot(chosen, wo, preferred_element_type=F32).astype(BF16)
    own = jnp.dot(picked(c, z, block), x_ref[...], preferred_element_type=F32)
    base_ref[...] = own + ob_ref[...][None, :]
    for copy in copies[7:]:
        copy.wait()


def pair_rows_kernel(n_z, block, keep_ref, got_ref, *outs):
    z = lax.axis_index("mp")
    for k in range(n_z):
        at = pl.ds(pl.multiple_of(lax.rem(z + k, n_z) * block, block), block)
        total = keep_ref[at, :].astype(F32) + got_ref[at, :].astype(F32)
        outs[k][...] = total.astype(outs[k].dtype)


def resid_kernel(base_ref, gain_ref, own_ref, *refs):
    out_ref = refs[-1]
    total = own_ref[...]
    for r in refs[:-1]:
        total += r[...].astype(F32)
    x = base_ref[...] + total
    scale = lax.rsqrt(jnp.mean(x * x, axis=-1, keepdims=True) + NORM_EPS)
    out_ref[...] = (x * scale * gain_ref[...][None, :]).astype(BF16)


def hidden_kernel(n_z, block, up_ref, ub_ref, *refs):
    c, z = lax.axis_index("section"), lax.axis_index("mp")
    pieces, (out_ref, xs) = refs[:2 * n_z], refs[2 * n_z:]
    width = xs.shape[2]
    for side in range(2):
        section = c if side == 0 else 1 - c
        for k in range(n_z):
            zz = lax.rem(z - k + n_z, n_z)
            chunk = chunk_of(section, zz, n_z)
            at = pl.ds(pl.multiple_of(chunk * block, block), block)
            xs[lax.rem(zz, JOIN), at, :] = pieces[side * n_z + k][...]
    acc = ub_ref[...][None, :]
    for q in range(JOIN):
        acc = acc + lax.dot_general(
            xs[q], up_ref[:, q * width:(q + 1) * width], NT, preferred_element_type=F32)
    out_ref[...] = (0.5 * acc * (1.0 + lax.erf(acc * (1.0 / math.sqrt(2.0))))).astype(BF16)


def down_kernel(other, hidden_ref, down_ref, out_ref):
    c = lax.axis_index("section")
    half = out_ref.shape[1]
    at = pl.ds(pl.multiple_of((1 - c if other else c) * half, half), half)
    out_ref[...] = jnp.dot(hidden_ref[...], down_ref[:, at], preferred_element_type=F32).astype(BF16)


def pair_columns_kernel(n_z, block, keep_ref, got_ref, *outs):
    z = lax.axis_index("mp")
    for k in range(n_z):
        at = pl.ds(pl.multiple_of(lax.rem(z + k, n_z) * block, block), block)
        total = keep_ref[:, at].astype(F32) + got_ref[:, at].astype(F32)
        outs[k][...] = total.astype(outs[k].dtype)


def image_kernel(n_z, bias_ref, own_ref, *refs):
    out_ref = refs[-1]
    block = out_ref.shape[1]
    d = lax.axis_index("section") * n_z + lax.axis_index("mp")
    total = own_ref[...]
    for r in refs[:-1]:
        total += r[...].astype(F32)
    at = pl.ds(pl.multiple_of(d * block, block), block)
    out_ref[...] = (total + bias_ref[at][None, :]).astype(BF16)


def image_keyval_kernel(n_z, text_ref, gain_ref, w_ref, b_ref, *refs):
    c, z = lax.axis_index("section"), lax.axis_index("mp")
    pieces, out_ref = refs[:-1], refs[-1]
    rows, block = pieces[0].shape
    prompt = text_ref.shape[0]
    out_ref[:prompt, :] = text_ref[...]
    acc = jnp.zeros((rows, out_ref.shape[1]), F32)
    squares = jnp.zeros((rows, 1), F32)
    for side in range(2):
        section = c if side == 0 else 1 - c
        for k in range(n_z):
            d = section * n_z + lax.rem(z - k + n_z, n_z)
            at = pl.ds(pl.multiple_of(d * block, block), block)
            x = pieces[side * n_z + k][...].astype(F32)
            squares += jnp.sum(x * x, axis=-1, keepdims=True)
            acc += jnp.dot((x * gain_ref[at][None, :]).astype(BF16), w_ref[at, :], preferred_element_type=F32)
    scale = lax.rsqrt(squares * (1.0 / w_ref.shape[0]) + NORM_EPS)
    out_ref[prompt:, :] = (acc * scale + b_ref[...][None, :]).astype(BF16)


def relay_kernel(n_z, linear, *refs):
    z = lax.axis_index("mp")
    pieces, out_ref = refs[:-1], refs[-1]
    if not linear:
        for k, piece in enumerate(pieces):
            out_ref[lax.rem(z - k + n_z, n_z)] = piece[...]
        return
    own, near, mid_first, mid_second, far_first, far_second = pieces
    low = z < 2
    out_ref[z] = own[...]
    out_ref[z + 1 - 2 * lax.rem(z, 2)] = near[...]
    inner = (z == 1) | (z == 2)
    out_ref[jnp.where(low, 2, 1)] = jnp.where(inner, mid_first[...], far_first[...])
    out_ref[jnp.where(low, 3, 0)] = jnp.where(inner, mid_second[...], far_second[...])


def text_keyval_kernel(gain_ref, w_ref, b_ref, here_ref, there_ref, out_ref):
    c = lax.axis_index("section")
    blocks, rows, model = here_ref.shape
    half = blocks * rows
    acc = jnp.zeros(out_ref.shape, F32)
    squares = jnp.zeros((out_ref.shape[0], 1), F32)
    step = 1024
    for first in range(0, model, step):
        at = slice(first, first + step)
        x = jnp.concatenate([r[i, :, at] for r in (here_ref, there_ref) for i in range(blocks)], axis=0).astype(F32)
        squares += jnp.sum(x * x, axis=-1, keepdims=True)
        y = (x * gain_ref[at][None, :]).astype(BF16)
        acc += jnp.dot(y, w_ref[at, :], preferred_element_type=F32)
    scale = lax.rsqrt(squares * (1.0 / model) + NORM_EPS)
    acc = (acc * scale + b_ref[...][None, :]).astype(BF16)
    out_ref[pl.ds(pl.multiple_of(c * half, half), half), :] = acc[:half]
    out_ref[pl.ds(pl.multiple_of((1 - c) * half, half), half), :] = acc[half:]


def place_kernel(n_s, slot_map, place_ref, *refs):
    s = lax.axis_index("seq")
    keyvals, (out_ref, held) = refs[:n_s], refs[n_s:]
    units = place_ref.shape[2]
    prompt = n_s * CTX
    for k in range(n_s):
        held[lax.rem(s - k + n_s, n_s)] = keyvals[k][prompt:, :]
    position = lax.broadcasted_iota(jnp.int32, (CTX, units), 0)
    for k in range(n_s):
        j = lax.rem(s - k + n_s, n_s)

        def one(i, carry):
            slot = slot_map[j, i] - s * n_s

            @pl.when((slot >= 0) & (slot < n_s))
            def _():
                chosen = position == place_ref[i, pl.ds(j, 1), :]
                covered = jnp.sum(chosen.astype(F32), axis=1, keepdims=True) > 0.5
                rows = held[i, pl.ds(pl.multiple_of(j * units, units), units), :]
                image = jnp.dot(chosen.astype(BF16), rows, preferred_element_type=F32)
                text = keyvals[k][pl.ds(pl.multiple_of(i * CTX, CTX), CTX), :]
                out_ref[slot] = jnp.where(covered, image, text.astype(F32)).astype(BF16)

            return carry

        lax.fori_loop(0, n_s, one, 0)


def shards(
    patches,
    image_place,
    slot_map,
    text,
    vision_gain,
    qkv_weight,
    qkv_bias,
    out_weight,
    out_bias,
    merge_gain,
    merge_up,
    merge_up_bias,
    merge_down,
    merge_down_bias,
    input_gain,
    kv_weight,
    kv_bias,
):
    n_z, n_s = lax.axis_size("mp"), lax.axis_size("seq")
    n_d = lax.axis_size("section") * n_z
    x = patches[0]
    rows, width = x.shape
    units = rows // JOIN
    block = rows // n_d
    head_width = out_weight.shape[0]
    model = merge_down.shape[1]
    columns = model // n_d
    kv_width = kv_weight.shape[1]

    def swap(v):
        return lax.ppermute(v, "section", [(0, 1), (1, 0)])

    def spread(own):
        here = [own] + [shifted(own, "mp", n_z, k) for k in range(1, n_z)]
        return here + [swap(v) for v in here]

    text_own = text[0]
    linear = n_z == 4
    if linear:
        def near(v):
            return lax.ppermute(v, "mp", [(0, 1), (1, 0), (2, 3), (3, 2)])

        def middle(v):
            return lax.ppermute(v, "mp", [(0, 0), (1, 2), (2, 1), (3, 3)])

        first = [near(text_own), middle(text_own)]
        second = [middle(first[0])]
        third = [near(first[1]), near(second[0])]
        text_pieces = [text_own, *first, *second, *third]
    else:
        text_pieces = [text_own] + [shifted(text_own, "mp", n_z, k) for k in range(1, n_z)]
        first, second = text_pieces[1:2], text_pieces[2:3]

    w = qkv_weight.transpose(1, 2, 0).reshape(3 * head_width, width)
    later = [merge_gain, merge_up.T, merge_up_bias, merge_down_bias, input_gain, kv_bias]
    keep, send, base, gain, up, up_bias, down_bias, text_gain, bias = call(
        functools.partial(front_kernel, n_z, block, len(later)),
        [struct((rows // 2, width), BF16)] * 2 + [struct((block, width), F32)]
        + [struct(v.shape, v.dtype) for v in later],
        [image_place, x, vision_gain, w, qkv_bias, out_weight, out_bias] + later,
        scratch=[
            pltpu.VMEM((rows, head_width), BF16), pltpu.SMEM(image_place.shape, jnp.int32),
            pltpu.VMEM(x.shape, BF16), pltpu.VMEM(vision_gain.shape, F32), pltpu.VMEM(w.shape, BF16),
            pltpu.VMEM(qkv_bias.shape, F32), pltpu.VMEM(out_weight.shape, BF16), pltpu.VMEM(out_bias.shape, F32),
            pltpu.SemaphoreType.DMA((7 + len(later),)),
        ],
        raw=True,
        grant=24,
        flops=2 * rows * width * 4 * head_width,
    )
    got = swap(send)
    parts = call(
        functools.partial(pair_rows_kernel, n_z, block),
        [struct((block, width), F32)] + [struct((block, width), BF16)] * (n_z - 1),
        [keep, got],
    )
    sums = [parts[0]] + [shifted(parts[k], "mp", n_z, k) for k in range(1, n_z)]
    merged, = call(
        resid_kernel, [struct((block, width), BF16)], [base, gain] + sums, after=first)
    pieces = spread(merged)

    hidden, = call(
        functools.partial(hidden_kernel, n_z, block),
        [struct((units, merge_up.shape[1]), BF16)],
        [up, up_bias] + pieces,
        scratch=[pltpu.VMEM((JOIN, units, width), BF16)],
        flops=2 * units * merge_up.size,
    )
    send, keep = (
        call(
            functools.partial(down_kernel, other),
            [struct((units, model // 2), BF16)],
            [hidden, merge_down],
            after=second if other else (),
            flops=units * merge_down.size,
            grant=16,
        )[0]
        for other in (True, False)
    )
    got = swap(send)
    parts = call(
        functools.partial(pair_columns_kernel, n_z, columns),
        [struct((units, columns), F32)] + [struct((units, columns), BF16)] * (n_z - 1),
        [keep, got],
    )
    sums = [parts[0]] + [shifted(parts[k], "mp", n_z, k) for k in range(1, n_z)]
    image, = call(
        functools.partial(image_kernel, n_z), [struct((units, columns), BF16)], [down_bias] + sums)
    image_pieces = spread(image)

    line, = call(
        functools.partial(relay_kernel, n_z, linear), [struct((n_z,) + text_own.shape, BF16)], text_pieces, after=[image])
    prompt = n_d * text.shape[1]
    text_keyval, = call(
        text_keyval_kernel,
        [struct((prompt, kv_width), BF16)],
        [text_gain, kv_weight, bias, line, swap(line)],
        flops=2 * prompt * model * kv_width,
        grant=16,
    )

    keyval, = call(
        functools.partial(image_keyval_kernel, n_z),
        [struct((prompt + units, kv_width), BF16)],
        [text_keyval, text_gain, kv_weight, bias] + image_pieces,
        flops=2 * units * model * kv_width,
        grant=16,
    )
    keyvals = [keyval] + [shifted(keyval, "seq", n_s, k) for k in range(1, n_s)]
    cache, = call(
        functools.partial(place_kernel, n_s),
        [struct((n_s, CTX, kv_width), BF16)],
        [slot_map, image_place] + keyvals,
        scratch=[pltpu.VMEM((n_s, units, kv_width), BF16)],
        smem=1,
        grant=16,
    )
    return cache[None]


def solution(mesh):
    placed = (
        P("seq", None, None),
        P(),
        P(),
        P("seq", ("section", "mp"), None),
        P(),
        P(None, None, ("section", "mp")),
        P(None, ("section", "mp")),
        P(("section", "mp"), None),
        P(),
        P(),
        P(None, ("section", "mp")),
        P(("section", "mp")),
        P(("section", "mp"), None),
        P(),
        P(),
        P(None, ("section", "mp")),
        P(("section", "mp")),
    )
    return jax.shard_map(
        shards,
        mesh=mesh,
        in_specs=placed,
        out_specs=P("section", "seq", None, "mp"),
        check_vma=False,
    )
```

```python
import functools
import math

import jax
import jax.numpy as jnp
from jax import lax
from jax.experimental import pallas as pl
from jax.experimental.pallas import tpu as pltpu
from jax.sharding import PartitionSpec as P

VHEAD = 80
CTX = 32
WIN = 64
JOIN = 4
NORM_EPS = 1e-06
F32 = jnp.float32
BF16 = jnp.bfloat16
MIB = 1024 * 1024
NT = (((1,), (1,)), ((), ()))


def call(kernel, outs, args, after=(), scratch=(), smem=0, raw=False, flops=0, grant=8):
    space = pl.BlockSpec(memory_space=pltpu.HBM if raw else pltpu.VMEM)
    scalar = pl.BlockSpec(memory_space=pltpu.SMEM)
    unread = pl.BlockSpec(memory_space=pl.ANY)
    moved = sum(math.prod(a.shape) * a.dtype.itemsize for a in list(args) + list(outs))
    count = len(after)
    if raw:
        args = [pltpu.with_memory_space_constraint(a, pltpu.HBM) for a in args]

    def body(*refs):
        kernel(*refs[count:])

    return pl.pallas_call(
        body,
        out_shape=outs,
        in_specs=[unread] * count + [scalar] * smem + [space] * (len(args) - smem),
        out_specs=[pl.BlockSpec(memory_space=pltpu.VMEM)] * len(outs),
        scratch_shapes=list(scratch),
        compiler_params=pltpu.CompilerParams(vmem_limit_bytes=grant * MIB),
        cost_estimate=pl.CostEstimate(flops=flops, bytes_accessed=moved, transcendentals=0),
    )(*after, *args)


def struct(shape, dtype):
    return jax.ShapeDtypeStruct(shape, dtype)


def shifted(x, axis, count, k):
    return lax.ppermute(x, axis, [(i, (i + k) % count) for i in range(count)])


def chunk_of(section, z, n_z):
    return section * (n_z // JOIN) + z // JOIN


def front_kernel(n_z, block, kept, place_hbm, x_hbm, gain_hbm, w_hbm, b_hbm, wo_hbm, ob_hbm, *refs):
    later, refs = refs[:kept], refs[kept:]
    (keep_ref, base_ref), sends, refs = refs[:2], refs[2:2 + n_z], refs[2 + n_z:]
    held, refs = refs[:kept], refs[kept:]
    hf, place, x_ref, gain_ref, w_ref, b_ref, wo_ref, ob_ref, sems = refs
    brought = (
        (x_hbm, x_ref), (gain_hbm, gain_ref), (w_hbm, w_ref), (b_hbm, b_ref),
        (place_hbm, place), (wo_hbm, wo_ref), (ob_hbm, ob_ref), *zip(later, held),
    )
    copies = [pltpu.make_async_copy(a, b, sems.at[i]) for i, (a, b) in enumerate(brought)]
    for copy in copies:
        copy.start()
    c, z, s = lax.axis_index("section"), lax.axis_index("mp"), lax.axis_index("seq")
    rows, width = x_ref.shape
    head_width = hf.shape[1]
    units = place.shape[2]
    tile = 256
    per_tile = tile // WIN
    for copy in copies[:5]:
        copy.wait()

    def one(t, carry):
        at = pl.ds(pl.multiple_of(t * tile, tile), tile)
        x = x_ref[at, :].astype(F32)
        scale = lax.rsqrt(jnp.mean(x * x, axis=-1, keepdims=True) + NORM_EPS)
        y = (x * scale * gain_ref[...][None, :]).astype(BF16)
        parts = []
        for i in range(3):
            w = w_ref[i * head_width:(i + 1) * head_width, :]
            part = lax.dot_general(y, w, NT, preferred_element_type=F32)
            parts.append((part + b_ref[i:i + 1, :]).astype(BF16))
        q, k, v = parts
        key = lax.broadcasted_iota(jnp.int32, (tile, tile), 1)
        row = lax.broadcasted_iota(jnp.int32, (tile, tile), 0)
        same = key // WIN == row // WIN
        end = jnp.zeros((tile, tile), jnp.int32)
        for j in range(per_tile):
            count = jnp.int32(0)
            for u in range(units):
                count += (place[s, t * per_tile + j, u] >= 0).astype(jnp.int32)
            end = jnp.where(key // WIN == j, j * WIN + count * JOIN, end)
        live = same & (key < end)
        lane = lax.broadcasted_iota(jnp.int32, (1, head_width), 1)
        total = jnp.zeros((tile, head_width), F32)
        for h in range(head_width // VHEAD):
            mine = lane // VHEAD == h
            qh = jnp.where(mine, q, jnp.zeros_like(q))
            scores = lax.dot_general(qh, k, NT, preferred_element_type=F32) * (1.0 / math.sqrt(VHEAD))
            raised = jnp.where(live, jnp.exp(scores), 0.0)
            probs = (raised / jnp.sum(raised, axis=-1, keepdims=True)).astype(BF16)
            out = jnp.dot(probs, v, preferred_element_type=F32)
            total = jnp.where(mine, out, total)
        hf[at, :] = total.astype(BF16)
        return carry

    if rows == tile:
        one(0, 0)
    else:
        lax.fori_loop(0, rows // tile, one, 0)

    def picked(section, zz, count):
        i = lax.broadcasted_iota(jnp.int32, (count, rows), 0)
        device = zz + i // block
        first = JOIN * block * chunk_of(section, device, n_z) + device % JOIN
        source = first + JOIN * (i % block)
        return (lax.broadcasted_iota(jnp.int32, (count, rows), 1) == source).astype(BF16)

    copies[5].wait()
    copies[6].wait()
    wo = wo_ref[...]
    heads = hf[...]
    def summed(section):
        chosen = jnp.dot(picked(section, 0, rows // 2), heads, preferred_element_type=F32).astype(BF16)
        return jnp.dot(chosen, wo, preferred_element_type=F32).astype(BF16)

    other = summed(1 - c)
    for zz, out in enumerate(sends):
        out[...] = other[zz * block:(zz + 1) * block, :]
    keep_ref[...] = summed(c)
    own = jnp.dot(picked(c, z, block), x_ref[...], preferred_element_type=F32)
    base_ref[...] = own + ob_ref[...][None, :]
    for copy in copies[7:]:
        copy.wait()


def pair_rows_kernel(n_z, block, keep_ref, *refs):
    z = lax.axis_index("mp")
    gots, outs = refs[:n_z], refs[n_z:]
    for k in range(n_z):
        mine = lax.rem(z + k, n_z)
        keep = keep_ref[pl.ds(pl.multiple_of(mine * block, block), block), :].astype(F32)
        for zz in range(n_z):

            @pl.when(mine == zz)
            def _():
                outs[k][...] = (keep + gots[zz][...].astype(F32)).astype(outs[k].dtype)


def resid_kernel(base_ref, gain_ref, own_ref, *refs):
    out_ref = refs[-1]
    total = own_ref[...]
    for r in refs[:-1]:
        total += r[...].astype(F32)
    x = base_ref[...] + total
    scale = lax.rsqrt(jnp.mean(x * x, axis=-1, keepdims=True) + NORM_EPS)
    out_ref[...] = (x * scale * gain_ref[...][None, :]).astype(BF16)


def hidden_kernel(n_z, block, up_ref, ub_ref, *refs):
    c, z = lax.axis_index("section"), lax.axis_index("mp")
    pieces, (out_ref, xs) = refs[:2 * n_z], refs[2 * n_z:]
    width = xs.shape[2]
    for side in range(2):
        section = c if side == 0 else 1 - c
        for k in range(n_z):
            zz = lax.rem(z - k + n_z, n_z)
            chunk = chunk_of(section, zz, n_z)
            at = pl.ds(pl.multiple_of(chunk * block, block), block)
            xs[lax.rem(zz, JOIN), at, :] = pieces[side * n_z + k][...]
    acc = ub_ref[...][None, :]
    for q in range(JOIN):
        acc = acc + lax.dot_general(
            xs[q], up_ref[:, q * width:(q + 1) * width], NT, preferred_element_type=F32)
    out_ref[...] = (0.5 * acc * (1.0 + lax.erf(acc * (1.0 / math.sqrt(2.0))))).astype(BF16)


def down_kernel(other, hidden_ref, down_ref, *outs):
    c = lax.axis_index("section")
    width = outs[0].shape[1]
    first = (1 - c if other else c) * len(outs) * width
    for i, out in enumerate(outs):
        at = pl.ds(pl.multiple_of(first + i * width, width), width)
        out[...] = jnp.dot(hidden_ref[...], down_ref[:, at], preferred_element_type=F32).astype(BF16)


def pair_columns_kernel(n_z, *refs):
    z = lax.axis_index("mp")
    keeps, gots, outs = refs[:n_z], refs[n_z:2 * n_z], refs[2 * n_z:]
    for k in range(n_z):
        mine = lax.rem(z + k, n_z)
        for zz in range(n_z):

            @pl.when(mine == zz)
            def _():
                total = keeps[zz][...].astype(F32) + gots[zz][...].astype(F32)
                outs[k][...] = total.astype(outs[k].dtype)


def image_kernel(n_z, bias_ref, own_ref, *refs):
    out_ref = refs[-1]
    block = out_ref.shape[1]
    d = lax.axis_index("section") * n_z + lax.axis_index("mp")
    total = own_ref[...]
    for r in refs[:-1]:
        total += r[...].astype(F32)
    at = pl.ds(pl.multiple_of(d * block, block), block)
    out_ref[...] = (total + bias_ref[at][None, :]).astype(BF16)


def image_keyval_kernel(n_z, text_ref, gain_ref, w_ref, b_ref, *refs):
    c, z = lax.axis_index("section"), lax.axis_index("mp")
    pieces, out_ref = refs[:-1], refs[-1]
    rows, block = pieces[0].shape
    prompt = text_ref.shape[0]
    out_ref[:prompt, :] = text_ref[...]
    acc = jnp.zeros((rows, out_ref.shape[1]), F32)
    squares = jnp.zeros((rows, 1), F32)
    for side in range(2):
        section = c if side == 0 else 1 - c
        for k in range(n_z):
            d = section * n_z + lax.rem(z - k + n_z, n_z)
            at = pl.ds(pl.multiple_of(d * block, block), block)
            x = pieces[side * n_z + k][...].astype(F32)
            squares += jnp.sum(x * x, axis=-1, keepdims=True)
            acc += jnp.dot((x * gain_ref[at][None, :]).astype(BF16), w_ref[at, :], preferred_element_type=F32)
    scale = lax.rsqrt(squares * (1.0 / w_ref.shape[0]) + NORM_EPS)
    out_ref[prompt:, :] = (acc * scale + b_ref[...][None, :]).astype(BF16)


def relay_kernel(n_z, linear, *refs):
    z = lax.axis_index("mp")
    pieces, out_ref = refs[:-1], refs[-1]
    if not linear:
        for k, piece in enumerate(pieces):
            out_ref[lax.rem(z - k + n_z, n_z)] = piece[...]
        return
    own, near, mid_first, mid_second, far_first, far_second = pieces
    low = z < 2
    out_ref[z] = own[...]
    out_ref[z + 1 - 2 * lax.rem(z, 2)] = near[...]
    inner = (z == 1) | (z == 2)
    out_ref[jnp.where(low, 2, 1)] = jnp.where(inner, mid_first[...], far_first[...])
    out_ref[jnp.where(low, 3, 0)] = jnp.where(inner, mid_second[...], far_second[...])


def text_keyval_kernel(gain_ref, w_ref, b_ref, here_ref, there_ref, out_ref):
    c = lax.axis_index("section")
    blocks, rows, model = here_ref.shape
    half = blocks * rows
    acc = jnp.zeros(out_ref.shape, F32)
    squares = jnp.zeros((out_ref.shape[0], 1), F32)
    step = 1024
    for first in range(0, model, step):
        at = slice(first, first + step)
        x = jnp.concatenate([r[i, :, at] for r in (here_ref, there_ref) for i in range(blocks)], axis=0).astype(F32)
        squares += jnp.sum(x * x, axis=-1, keepdims=True)
        y = (x * gain_ref[at][None, :]).astype(BF16)
        acc += jnp.dot(y, w_ref[at, :], preferred_element_type=F32)
    scale = lax.rsqrt(squares * (1.0 / model) + NORM_EPS)
    acc = (acc * scale + b_ref[...][None, :]).astype(BF16)
    out_ref[pl.ds(pl.multiple_of(c * half, half), half), :] = acc[:half]
    out_ref[pl.ds(pl.multiple_of((1 - c) * half, half), half), :] = acc[half:]


def place_kernel(n_s, slot_map, place_ref, *refs):
    s = lax.axis_index("seq")
    keyvals, (out_ref, held, texts) = refs[:n_s], refs[n_s:]
    units = place_ref.shape[2]
    prompt = n_s * CTX
    for k in range(n_s):
        held[lax.rem(s - k + n_s, n_s)] = keyvals[k][prompt:, :]
    position = lax.broadcasted_iota(jnp.int32, (CTX, units), 0)
    for k in range(n_s):
        texts[lax.rem(s - k + n_s, n_s)] = keyvals[k][:prompt, :]

    def source(t):
        def look(n, found):
            return jnp.where(slot_map[n // n_s, n % n_s] == s * n_s + t, n, found)

        found = lax.fori_loop(0, n_s * n_s, look, 0, unroll=n_s == 4)
        return found // n_s, found % n_s

    def one(t):
        j, i = source(t)
        chosen = position == place_ref[i, pl.ds(j, 1), :]
        covered = jnp.sum(chosen.astype(F32), axis=1, keepdims=True) > 0.5
        rows = held[i, pl.ds(pl.multiple_of(j * units, units), units), :]
        image = jnp.dot(chosen.astype(BF16), rows, preferred_element_type=F32)
        text = texts[j, pl.ds(pl.multiple_of(i * CTX, CTX), CTX), :]
        out_ref[t] = jnp.where(covered, image, text.astype(F32)).astype(BF16)

    for t in range(n_s):
        one(t)


def shards(
    patches,
    image_place,
    slot_map,
    text,
    vision_gain,
    qkv_weight,
    qkv_bias,
    out_weight,
    out_bias,
    merge_gain,
    merge_up,
    merge_up_bias,
    merge_down,
    merge_down_bias,
    input_gain,
    kv_weight,
    kv_bias,
):
    n_z, n_s = lax.axis_size("mp"), lax.axis_size("seq")
    n_d = lax.axis_size("section") * n_z
    x = patches[0]
    rows, width = x.shape
    units = rows // JOIN
    block = rows // n_d
    head_width = out_weight.shape[0]
    model = merge_down.shape[1]
    columns = model // n_d
    kv_width = kv_weight.shape[1]

    def swap(v):
        return lax.ppermute(v, "section", [(0, 1), (1, 0)])

    def spread(own):
        here = [own] + [shifted(own, "mp", n_z, k) for k in range(1, n_z)]
        return here + [swap(v) for v in here]

    text_own = text[0]
    linear = n_z == 4
    if linear:
        def near(v):
            return lax.ppermute(v, "mp", [(0, 1), (1, 0), (2, 3), (3, 2)])

        def middle(v):
            return lax.ppermute(v, "mp", [(0, 0), (1, 2), (2, 1), (3, 3)])

        near_own, middle_own = near(text_own), middle(text_own)
        middle_near, near_middle = middle(near_own), near(middle_own)
        near_last = near(middle_near)
        text_pieces = [text_own, near_own, middle_own, middle_near, near_middle, near_last]
    else:
        text_pieces = [text_own] + [shifted(text_own, "mp", n_z, k) for k in range(1, n_z)]

    w = qkv_weight.transpose(1, 2, 0).reshape(3 * head_width, width)
    later = [merge_gain, merge_up.T, merge_up_bias, merge_down_bias, input_gain, kv_bias]
    keep, base, *rest = call(
        functools.partial(front_kernel, n_z, block, len(later)),
        [struct((rows // 2, width), BF16), struct((block, width), F32)]
        + [struct((block, width), BF16)] * n_z
        + [struct(v.shape, v.dtype) for v in later],
        [image_place, x, vision_gain, w, qkv_bias, out_weight, out_bias] + later,
        scratch=[
            pltpu.VMEM((rows, head_width), BF16), pltpu.SMEM(image_place.shape, jnp.int32),
            pltpu.VMEM(x.shape, BF16), pltpu.VMEM(vision_gain.shape, F32), pltpu.VMEM(w.shape, BF16),
            pltpu.VMEM(qkv_bias.shape, F32), pltpu.VMEM(out_weight.shape, BF16), pltpu.VMEM(out_bias.shape, F32),
            pltpu.SemaphoreType.DMA((7 + len(later),)),
        ],
        raw=True,
        grant=24,
        flops=2 * rows * width * 4 * head_width,
    )
    sends, (gain, up, up_bias, down_bias, text_gain, bias) = rest[:n_z], rest[n_z:]
    parts = call(
        functools.partial(pair_rows_kernel, n_z, block),
        [struct((block, width), F32)] + [struct((block, width), BF16)] * (n_z - 1),
        [keep] + [swap(v) for v in sends],
    )
    sums = [parts[0]] + [shifted(parts[k], "mp", n_z, k) for k in range(1, n_z)]
    merged, = call(
        resid_kernel, [struct((block, width), BF16)], [base, gain] + sums)
    pieces = spread(merged)

    hidden, = call(
        functools.partial(hidden_kernel, n_z, block),
        [struct((units, merge_up.shape[1]), BF16)],
        [up, up_bias] + pieces,
        scratch=[pltpu.VMEM((JOIN, units, width), BF16)],
        flops=2 * units * merge_up.size,
    )
    sends, keeps = (
        call(
            functools.partial(down_kernel, other),
            [struct((units, columns), BF16)] * n_z,
            [hidden, merge_down],
            flops=units * merge_down.size,
            grant=16,
        )
        for other in (True, False)
    )
    parts = call(
        functools.partial(pair_columns_kernel, n_z),
        [struct((units, columns), F32)] + [struct((units, columns), BF16)] * (n_z - 1),
        [*keeps, *(swap(v) for v in sends)],
    )
    sums = [parts[0]] + [shifted(parts[k], "mp", n_z, k) for k in range(1, n_z)]
    image, = call(
        functools.partial(image_kernel, n_z), [struct((units, columns), BF16)], [down_bias] + sums)
    image_pieces = spread(image)

    line, = call(
        functools.partial(relay_kernel, n_z, linear), [struct((n_z,) + text_own.shape, BF16)], text_pieces, after=[image])
    prompt = n_d * text.shape[1]
    text_keyval, = call(
        text_keyval_kernel,
        [struct((prompt, kv_width), BF16)],
        [text_gain, kv_weight, bias, line, swap(line)],
        flops=2 * prompt * model * kv_width,
        grant=16,
    )

    keyval, = call(
        functools.partial(image_keyval_kernel, n_z),
        [struct((prompt + units, kv_width), BF16)],
        [text_keyval, text_gain, kv_weight, bias] + image_pieces,
        flops=2 * units * model * kv_width,
        grant=16,
    )
    keyvals = [keyval] + [shifted(keyval, "seq", n_s, k) for k in range(1, n_s)]
    cache, = call(
        functools.partial(place_kernel, n_s),
        [struct((n_s, CTX, kv_width), BF16)],
        [slot_map, image_place] + keyvals,
        scratch=[pltpu.VMEM((n_s, units, kv_width), BF16), pltpu.VMEM((n_s, prompt, kv_width), BF16)],
        smem=1,
        grant=16,
    )
    return cache[None]


def solution(mesh):
    placed = (
        P("seq", None, None),
        P(),
        P(),
        P("seq", ("section", "mp"), None),
        P(),
        P(None, None, ("section", "mp")),
        P(None, ("section", "mp")),
        P(("section", "mp"), None),
        P(),
        P(),
        P(None, ("section", "mp")),
        P(("section", "mp")),
        P(("section", "mp"), None),
        P(),
        P(),
        P(None, ("section", "mp")),
        P(("section", "mp")),
    )
    return jax.shard_map(
        shards,
        mesh=mesh,
        in_specs=placed,
        out_specs=P("section", "seq", None, "mp"),
        check_vma=False,
    )
```

```python
import functools
import math

import jax
import jax.numpy as jnp
from jax import lax
from jax.experimental import pallas as pl
from jax.experimental.pallas import tpu as pltpu
from jax.sharding import PartitionSpec as P

VHEAD = 80
CTX = 32
WIN = 64
JOIN = 4
NORM_EPS = 1e-06
F32 = jnp.float32
BF16 = jnp.bfloat16
MIB = 1024 * 1024
NT = (((1,), (1,)), ((), ()))


def call(kernel, outs, args, after=(), scratch=(), smem=0, raw=False, flops=0, grant=8):
    space = pl.BlockSpec(memory_space=pltpu.HBM if raw else pltpu.VMEM)
    scalar = pl.BlockSpec(memory_space=pltpu.SMEM)
    unread = pl.BlockSpec(memory_space=pl.ANY)
    moved = sum(math.prod(a.shape) * a.dtype.itemsize for a in list(args) + list(outs))
    count = len(after)
    if raw:
        args = [pltpu.with_memory_space_constraint(a, pltpu.HBM) for a in args]

    def body(*refs):
        kernel(*refs[count:])

    return pl.pallas_call(
        body,
        out_shape=outs,
        in_specs=[unread] * count + [scalar] * smem + [space] * (len(args) - smem),
        out_specs=[pl.BlockSpec(memory_space=pltpu.VMEM)] * len(outs),
        scratch_shapes=list(scratch),
        compiler_params=pltpu.CompilerParams(vmem_limit_bytes=grant * MIB),
        cost_estimate=pl.CostEstimate(flops=flops, bytes_accessed=moved, transcendentals=0),
    )(*after, *args)


def struct(shape, dtype):
    return jax.ShapeDtypeStruct(shape, dtype)


def shifted(x, axis, count, k):
    return lax.ppermute(x, axis, [(i, (i + k) % count) for i in range(count)])


def chunk_of(section, z, n_z):
    return section * (n_z // JOIN) + z // JOIN


def front_kernel(n_z, block, kept, place_hbm, x_hbm, gain_hbm, w_hbm, b_hbm, wo_hbm, ob_hbm, *refs):
    later, refs = refs[:kept], refs[kept:]
    (keep_ref, base_ref), sends, refs = refs[:2], refs[2:2 + n_z], refs[2 + n_z:]
    held, refs = refs[:kept], refs[kept:]
    hf, place, x_ref, gain_ref, w_ref, b_ref, wo_ref, ob_ref, sems = refs
    brought = (
        (x_hbm, x_ref), (gain_hbm, gain_ref), (w_hbm, w_ref), (b_hbm, b_ref),
        (place_hbm, place), (wo_hbm, wo_ref), (ob_hbm, ob_ref), *zip(later, held),
    )
    copies = [pltpu.make_async_copy(a, b, sems.at[i]) for i, (a, b) in enumerate(brought)]
    for copy in copies:
        copy.start()
    c, z, s = lax.axis_index("section"), lax.axis_index("mp"), lax.axis_index("seq")
    rows, width = x_ref.shape
    head_width = hf.shape[1]
    units = place.shape[2]
    tile = 256
    per_tile = tile // WIN
    for copy in copies[:5]:
        copy.wait()

    def one(t, carry):
        at = pl.ds(pl.multiple_of(t * tile, tile), tile)
        x = x_ref[at, :].astype(F32)
        scale = lax.rsqrt(jnp.mean(x * x, axis=-1, keepdims=True) + NORM_EPS)
        y = (x * scale * gain_ref[...][None, :]).astype(BF16)
        parts = []
        for i in range(3):
            w = w_ref[i * head_width:(i + 1) * head_width, :]
            part = lax.dot_general(y, w, NT, preferred_element_type=F32)
            parts.append((part + b_ref[i:i + 1, :]).astype(BF16))
        q, k, v = parts
        key = lax.broadcasted_iota(jnp.int32, (tile, tile), 1)
        row = lax.broadcasted_iota(jnp.int32, (tile, tile), 0)
        same = key // WIN == row // WIN
        end = jnp.zeros((tile, tile), jnp.int32)
        for j in range(per_tile):
            count = jnp.int32(0)
            for u in range(units):
                count += (place[s, t * per_tile + j, u] >= 0).astype(jnp.int32)
            end = jnp.where(key // WIN == j, j * WIN + count * JOIN, end)
        live = same & (key < end)
        lane = lax.broadcasted_iota(jnp.int32, (1, head_width), 1)
        total = jnp.zeros((tile, head_width), F32)
        for h in range(head_width // VHEAD):
            mine = lane // VHEAD == h
            qh = jnp.where(mine, q, jnp.zeros_like(q))
            scores = lax.dot_general(qh, k, NT, preferred_element_type=F32) * (1.0 / math.sqrt(VHEAD))
            raised = jnp.where(live, jnp.exp(scores), 0.0)
            probs = (raised / jnp.sum(raised, axis=-1, keepdims=True)).astype(BF16)
            out = jnp.dot(probs, v, preferred_element_type=F32)
            total = jnp.where(mine, out, total)
        hf[at, :] = total.astype(BF16)
        return carry

    if rows == tile:
        one(0, 0)
    else:
        lax.fori_loop(0, rows // tile, one, 0)

    def picked(section, zz, count):
        i = lax.broadcasted_iota(jnp.int32, (count, rows), 0)
        device = zz + i // block
        first = JOIN * block * chunk_of(section, device, n_z) + device % JOIN
        source = first + JOIN * (i % block)
        return (lax.broadcasted_iota(jnp.int32, (count, rows), 1) == source).astype(BF16)

    copies[5].wait()
    copies[6].wait()
    wo = wo_ref[...]
    heads = hf[...]
    def summed(section):
        chosen = jnp.dot(picked(section, 0, rows // 2), heads, preferred_element_type=F32).astype(BF16)
        return jnp.dot(chosen, wo, preferred_element_type=F32).astype(BF16)

    other = summed(1 - c)
    for zz, out in enumerate(sends):
        out[...] = other[zz * block:(zz + 1) * block, :]
    keep_ref[...] = summed(c)
    own = jnp.dot(picked(c, z, block), x_ref[...], preferred_element_type=F32)
    base_ref[...] = own + ob_ref[...][None, :]
    for copy in copies[7:]:
        copy.wait()


def pair_rows_kernel(n_z, block, keep_ref, *refs):
    z = lax.axis_index("mp")
    gots, outs = refs[:n_z], refs[n_z:]
    for k in range(n_z):
        mine = lax.rem(z + k, n_z)
        keep = keep_ref[pl.ds(pl.multiple_of(mine * block, block), block), :].astype(F32)
        for zz in range(n_z):

            @pl.when(mine == zz)
            def _():
                outs[k][...] = (keep + gots[zz][...].astype(F32)).astype(outs[k].dtype)


def resid_kernel(base_ref, gain_ref, own_ref, *refs):
    out_ref = refs[-1]
    total = own_ref[...]
    for r in refs[:-1]:
        total += r[...].astype(F32)
    x = base_ref[...] + total
    scale = lax.rsqrt(jnp.mean(x * x, axis=-1, keepdims=True) + NORM_EPS)
    out_ref[...] = (x * scale * gain_ref[...][None, :]).astype(BF16)


def hidden_kernel(n_z, block, up_ref, ub_ref, *refs):
    c, z = lax.axis_index("section"), lax.axis_index("mp")
    pieces, (out_ref, xs) = refs[:2 * n_z], refs[2 * n_z:]
    width = xs.shape[2]
    for side in range(2):
        section = c if side == 0 else 1 - c
        for k in range(n_z):
            zz = lax.rem(z - k + n_z, n_z)
            chunk = chunk_of(section, zz, n_z)
            at = pl.ds(pl.multiple_of(chunk * block, block), block)
            xs[lax.rem(zz, JOIN), at, :] = pieces[side * n_z + k][...]
    acc = ub_ref[...][None, :]
    for q in range(JOIN):
        acc = acc + lax.dot_general(
            xs[q], up_ref[:, q * width:(q + 1) * width], NT, preferred_element_type=F32)
    out_ref[...] = (0.5 * acc * (1.0 + lax.erf(acc * (1.0 / math.sqrt(2.0))))).astype(BF16)


def down_kernel(other, hidden_ref, down_ref, *outs):
    c = lax.axis_index("section")
    width = outs[0].shape[1]
    first = (1 - c if other else c) * len(outs) * width
    for i, out in enumerate(outs):
        at = pl.ds(pl.multiple_of(first + i * width, width), width)
        out[...] = jnp.dot(hidden_ref[...], down_ref[:, at], preferred_element_type=F32).astype(BF16)


def pair_columns_kernel(n_z, *refs):
    z = lax.axis_index("mp")
    keeps, gots, outs = refs[:n_z], refs[n_z:2 * n_z], refs[2 * n_z:]
    for k in range(n_z):
        mine = lax.rem(z + k, n_z)
        for zz in range(n_z):

            @pl.when(mine == zz)
            def _():
                total = keeps[zz][...].astype(F32) + gots[zz][...].astype(F32)
                outs[k][...] = total.astype(outs[k].dtype)


def image_kernel(n_z, bias_ref, own_ref, *refs):
    out_ref = refs[-1]
    block = out_ref.shape[1]
    d = lax.axis_index("section") * n_z + lax.axis_index("mp")
    total = own_ref[...]
    for r in refs[:-1]:
        total += r[...].astype(F32)
    at = pl.ds(pl.multiple_of(d * block, block), block)
    out_ref[...] = (total + bias_ref[at][None, :]).astype(BF16)


def image_keyval_kernel(n_z, text_ref, gain_ref, w_ref, b_ref, *refs):
    c, z = lax.axis_index("section"), lax.axis_index("mp")
    pieces, out_ref = refs[:-1], refs[-1]
    rows, block = pieces[0].shape
    prompt = text_ref.shape[0]
    out_ref[:prompt, :] = text_ref[...]
    acc = jnp.zeros((rows, out_ref.shape[1]), F32)
    squares = jnp.zeros((rows, 1), F32)
    for side in range(2):
        section = c if side == 0 else 1 - c
        for k in range(n_z):
            d = section * n_z + lax.rem(z - k + n_z, n_z)
            at = pl.ds(pl.multiple_of(d * block, block), block)
            x = pieces[side * n_z + k][...].astype(F32)
            squares += jnp.sum(x * x, axis=-1, keepdims=True)
            acc += jnp.dot((x * gain_ref[at][None, :]).astype(BF16), w_ref[at, :], preferred_element_type=F32)
    scale = lax.rsqrt(squares * (1.0 / w_ref.shape[0]) + NORM_EPS)
    out_ref[prompt:, :] = (acc * scale + b_ref[...][None, :]).astype(BF16)


def relay_kernel(n_z, linear, *refs):
    z = lax.axis_index("mp")
    pieces, out_ref = refs[:-1], refs[-1]
    if not linear:
        for k, piece in enumerate(pieces):
            out_ref[lax.rem(z - k + n_z, n_z)] = piece[...]
        return
    pair = 1 - 2 * lax.rem(z, 2)
    far = lax.rem(z + 2, n_z)
    for at, piece in zip((z, z + pair, far, far + pair), pieces):
        out_ref[at] = piece[...]


def text_keyval_kernel(gain_ref, w_ref, b_ref, here_ref, there_ref, out_ref):
    c = lax.axis_index("section")
    blocks, rows, model = here_ref.shape
    half = blocks * rows
    acc = jnp.zeros(out_ref.shape, F32)
    squares = jnp.zeros((out_ref.shape[0], 1), F32)
    step = 1024
    for first in range(0, model, step):
        at = slice(first, first + step)
        x = jnp.concatenate([r[i, :, at] for r in (here_ref, there_ref) for i in range(blocks)], axis=0).astype(F32)
        squares += jnp.sum(x * x, axis=-1, keepdims=True)
        y = (x * gain_ref[at][None, :]).astype(BF16)
        acc += jnp.dot(y, w_ref[at, :], preferred_element_type=F32)
    scale = lax.rsqrt(squares * (1.0 / model) + NORM_EPS)
    acc = (acc * scale + b_ref[...][None, :]).astype(BF16)
    out_ref[pl.ds(pl.multiple_of(c * half, half), half), :] = acc[:half]
    out_ref[pl.ds(pl.multiple_of((1 - c) * half, half), half), :] = acc[half:]


def place_kernel(n_s, slot_map, place_ref, *refs):
    s = lax.axis_index("seq")
    keyvals, (out_ref, held, texts) = refs[:n_s], refs[n_s:]
    units = place_ref.shape[2]
    prompt = n_s * CTX
    for k in range(n_s):
        held[lax.rem(s - k + n_s, n_s)] = keyvals[k][prompt:, :]
    position = lax.broadcasted_iota(jnp.int32, (CTX, units), 0)
    for k in range(n_s):
        texts[lax.rem(s - k + n_s, n_s)] = keyvals[k][:prompt, :]

    def source(t):
        def look(n, found):
            return jnp.where(slot_map[n // n_s, n % n_s] == s * n_s + t, n, found)

        found = lax.fori_loop(0, n_s * n_s, look, 0, unroll=n_s == 4)
        return found // n_s, found % n_s

    def one(t):
        j, i = source(t)
        chosen = position == place_ref[i, pl.ds(j, 1), :]
        covered = jnp.sum(chosen.astype(F32), axis=1, keepdims=True) > 0.5
        rows = held[i, pl.ds(pl.multiple_of(j * units, units), units), :]
        image = jnp.dot(chosen.astype(BF16), rows, preferred_element_type=F32)
        text = texts[j, pl.ds(pl.multiple_of(i * CTX, CTX), CTX), :]
        out_ref[t] = jnp.where(covered, image, text.astype(F32)).astype(BF16)

    for t in range(n_s):
        one(t)


def shards(
    patches,
    image_place,
    slot_map,
    text,
    vision_gain,
    qkv_weight,
    qkv_bias,
    out_weight,
    out_bias,
    merge_gain,
    merge_up,
    merge_up_bias,
    merge_down,
    merge_down_bias,
    input_gain,
    kv_weight,
    kv_bias,
):
    n_z, n_s = lax.axis_size("mp"), lax.axis_size("seq")
    n_d = lax.axis_size("section") * n_z
    x = patches[0]
    rows, width = x.shape
    units = rows // JOIN
    block = rows // n_d
    head_width = out_weight.shape[0]
    model = merge_down.shape[1]
    columns = model // n_d
    kv_width = kv_weight.shape[1]

    def swap(v):
        return lax.ppermute(v, "section", [(0, 1), (1, 0)])

    def spread(own):
        here = [own] + [shifted(own, "mp", n_z, k) for k in range(1, n_z)]
        return here + [swap(v) for v in here]

    text_own = text[0]
    linear = n_z == 4
    if linear:
        def near(v):
            return lax.ppermute(v, "mp", [(0, 1), (1, 0), (2, 3), (3, 2)])

        def across(v):
            return lax.ppermute(v, "mp", [(0, 2), (2, 0), (1, 3), (3, 1)])

        across_own, near_own = across(text_own), near(text_own)
        near_across = near(across_own)
        text_pieces = [text_own, near_own, across_own, near_across]
        early, late = [across_own, near_own], [near_across]
    else:
        text_pieces = [text_own] + [shifted(text_own, "mp", n_z, k) for k in range(1, n_z)]
        early, late = text_pieces[1:2], text_pieces[2:3]

    w = qkv_weight.transpose(1, 2, 0).reshape(3 * head_width, width)
    later = [merge_gain, merge_up.T, merge_up_bias, merge_down_bias, input_gain, kv_bias]
    keep, base, *rest = call(
        functools.partial(front_kernel, n_z, block, len(later)),
        [struct((rows // 2, width), BF16), struct((block, width), F32)]
        + [struct((block, width), BF16)] * n_z
        + [struct(v.shape, v.dtype) for v in later],
        [image_place, x, vision_gain, w, qkv_bias, out_weight, out_bias] + later,
        scratch=[
            pltpu.VMEM((rows, head_width), BF16), pltpu.SMEM(image_place.shape, jnp.int32),
            pltpu.VMEM(x.shape, BF16), pltpu.VMEM(vision_gain.shape, F32), pltpu.VMEM(w.shape, BF16),
            pltpu.VMEM(qkv_bias.shape, F32), pltpu.VMEM(out_weight.shape, BF16), pltpu.VMEM(out_bias.shape, F32),
            pltpu.SemaphoreType.DMA((7 + len(later),)),
        ],
        raw=True,
        grant=24,
        flops=2 * rows * width * 4 * head_width,
    )
    sends, (gain, up, up_bias, down_bias, text_gain, bias) = rest[:n_z], rest[n_z:]
    parts = call(
        functools.partial(pair_rows_kernel, n_z, block),
        [struct((block, width), F32)] + [struct((block, width), BF16)] * (n_z - 1),
        [keep] + [swap(v) for v in sends],
    )
    sums = [parts[0]] + [shifted(parts[k], "mp", n_z, k) for k in range(1, n_z)]
    merged, = call(
        resid_kernel, [struct((block, width), BF16)], [base, gain] + sums, after=early)
    pieces = spread(merged)

    hidden, = call(
        functools.partial(hidden_kernel, n_z, block),
        [struct((units, merge_up.shape[1]), BF16)],
        [up, up_bias] + pieces,
        scratch=[pltpu.VMEM((JOIN, units, width), BF16)],
        flops=2 * units * merge_up.size,
    )
    sends, keeps = (
        call(
            functools.partial(down_kernel, other),
            [struct((units, columns), BF16)] * n_z,
            [hidden, merge_down],
            after=late if other else (),
            flops=units * merge_down.size,
            grant=16,
        )
        for other in (True, False)
    )
    parts = call(
        functools.partial(pair_columns_kernel, n_z),
        [struct((units, columns), F32)] + [struct((units, columns), BF16)] * (n_z - 1),
        [*keeps, *(swap(v) for v in sends)],
    )
    sums = [parts[0]] + [shifted(parts[k], "mp", n_z, k) for k in range(1, n_z)]
    image, = call(
        functools.partial(image_kernel, n_z), [struct((units, columns), BF16)], [down_bias] + sums)
    image_pieces = spread(image)

    line, = call(
        functools.partial(relay_kernel, n_z, linear), [struct((n_z,) + text_own.shape, BF16)], text_pieces, after=[image])
    prompt = n_d * text.shape[1]
    text_keyval, = call(
        text_keyval_kernel,
        [struct((prompt, kv_width), BF16)],
        [text_gain, kv_weight, bias, line, swap(line)],
        flops=2 * prompt * model * kv_width,
        grant=16,
    )

    keyval, = call(
        functools.partial(image_keyval_kernel, n_z),
        [struct((prompt + units, kv_width), BF16)],
        [text_keyval, text_gain, kv_weight, bias] + image_pieces,
        flops=2 * units * model * kv_width,
        grant=16,
    )
    keyvals = [keyval] + [shifted(keyval, "seq", n_s, k) for k in range(1, n_s)]
    cache, = call(
        functools.partial(place_kernel, n_s),
        [struct((n_s, CTX, kv_width), BF16)],
        [slot_map, image_place] + keyvals,
        scratch=[pltpu.VMEM((n_s, units, kv_width), BF16), pltpu.VMEM((n_s, prompt, kv_width), BF16)],
        smem=1,
        grant=16,
    )
    return cache[None]


def solution(mesh):
    placed = (
        P("seq", None, None),
        P(),
        P(),
        P("seq", ("section", "mp"), None),
        P(),
        P(None, None, ("section", "mp")),
        P(None, ("section", "mp")),
        P(("section", "mp"), None),
        P(),
        P(),
        P(None, ("section", "mp")),
        P(("section", "mp")),
        P(("section", "mp"), None),
        P(),
        P(),
        P(None, ("section", "mp")),
        P(("section", "mp")),
    )
    return jax.shard_map(
        shards,
        mesh=mesh,
        in_specs=placed,
        out_specs=P("section", "seq", None, "mp"),
        check_vma=False,
    )
```

```python
import functools
import math

import jax
import jax.numpy as jnp
from jax import lax
from jax.experimental import pallas as pl
from jax.experimental.pallas import tpu as pltpu
from jax.sharding import PartitionSpec as P

VHEAD = 80
CTX = 32
WIN = 64
JOIN = 4
NORM_EPS = 1e-06
F32 = jnp.float32
BF16 = jnp.bfloat16
MIB = 1024 * 1024
NT = (((1,), (1,)), ((), ()))


def call(kernel, outs, args, after=(), scratch=(), smem=0, raw=False, flops=0, grant=8):
    space = pl.BlockSpec(memory_space=pltpu.HBM if raw else pltpu.VMEM)
    scalar = pl.BlockSpec(memory_space=pltpu.SMEM)
    unread = pl.BlockSpec(memory_space=pl.ANY)
    moved = sum(math.prod(a.shape) * a.dtype.itemsize for a in list(args) + list(outs))
    count = len(after)
    if raw:
        args = [pltpu.with_memory_space_constraint(a, pltpu.HBM) for a in args]

    def body(*refs):
        kernel(*refs[count:])

    return pl.pallas_call(
        body,
        out_shape=outs,
        in_specs=[unread] * count + [scalar] * smem + [space] * (len(args) - smem),
        out_specs=[pl.BlockSpec(memory_space=pltpu.VMEM)] * len(outs),
        scratch_shapes=list(scratch),
        compiler_params=pltpu.CompilerParams(vmem_limit_bytes=grant * MIB),
        cost_estimate=pl.CostEstimate(flops=flops, bytes_accessed=moved, transcendentals=0),
    )(*after, *args)


def struct(shape, dtype):
    return jax.ShapeDtypeStruct(shape, dtype)


def shifted(x, axis, count, k):
    return lax.ppermute(x, axis, [(i, (i + k) % count) for i in range(count)])


def origin(z, k, n_z):
    return lax.rem(z - k + n_z, n_z)


def chunk_of(section, z, n_z):
    return section * (n_z // JOIN) + z // JOIN


def front_kernel(n_z, block, kept, place_hbm, x_hbm, gain_hbm, w_hbm, b_hbm, wo_hbm, ob_hbm, *refs):
    later, refs = refs[:kept], refs[kept:]
    (keep_ref, base_ref), sends, refs = refs[:2], refs[2:2 + n_z], refs[2 + n_z:]
    held, refs = refs[:kept], refs[kept:]
    hf, place, x_ref, gain_ref, w_ref, b_ref, wo_ref, ob_ref, sems = refs
    brought = (
        (x_hbm, x_ref), (gain_hbm, gain_ref), (w_hbm, w_ref), (b_hbm, b_ref),
        (place_hbm, place), (wo_hbm, wo_ref), (ob_hbm, ob_ref), *zip(later, held),
    )
    copies = [pltpu.make_async_copy(a, b, sems.at[i]) for i, (a, b) in enumerate(brought)]
    for copy in copies:
        copy.start()
    c, z, s = lax.axis_index("section"), lax.axis_index("mp"), lax.axis_index("seq")
    rows, width = x_ref.shape
    head_width = hf.shape[1]
    units = place.shape[2]
    tile = 256
    per_tile = tile // WIN
    for copy in copies[:5]:
        copy.wait()

    def one(t, carry):
        at = pl.ds(pl.multiple_of(t * tile, tile), tile)
        x = x_ref[at, :].astype(F32)
        scale = lax.rsqrt(jnp.mean(x * x, axis=-1, keepdims=True) + NORM_EPS)
        y = (x * scale * gain_ref[...][None, :]).astype(BF16)
        parts = []
        for i in range(3):
            w = w_ref[i * head_width:(i + 1) * head_width, :]
            part = lax.dot_general(y, w, NT, preferred_element_type=F32)
            parts.append((part + b_ref[i:i + 1, :]).astype(BF16))
        q, k, v = parts
        key = lax.broadcasted_iota(jnp.int32, (tile, tile), 1)
        row = lax.broadcasted_iota(jnp.int32, (tile, tile), 0)
        same = key // WIN == row // WIN
        end = jnp.zeros((tile, tile), jnp.int32)
        for j in range(per_tile):
            count = jnp.int32(0)
            for u in range(units):
                count += (place[s, t * per_tile + j, u] >= 0).astype(jnp.int32)
            end = jnp.where(key // WIN == j, j * WIN + count * JOIN, end)
        live = same & (key < end)
        lane = lax.broadcasted_iota(jnp.int32, (1, head_width), 1)
        total = jnp.zeros((tile, head_width), F32)
        for h in range(head_width // VHEAD):
            mine = lane // VHEAD == h
            qh = jnp.where(mine, q, jnp.zeros_like(q))
            scores = lax.dot_general(qh, k, NT, preferred_element_type=F32) * (1.0 / math.sqrt(VHEAD))
            raised = jnp.where(live, jnp.exp(scores), 0.0)
            probs = (raised / jnp.sum(raised, axis=-1, keepdims=True)).astype(BF16)
            out = jnp.dot(probs, v, preferred_element_type=F32)
            total = jnp.where(mine, out, total)
        hf[at, :] = total.astype(BF16)
        return carry

    if rows == tile:
        one(0, 0)
    else:
        lax.fori_loop(0, rows // tile, one, 0)

    def picked(section, zz, count):
        i = lax.broadcasted_iota(jnp.int32, (count, rows), 0)
        device = zz + i // block
        first = JOIN * block * chunk_of(section, device, n_z) + device % JOIN
        source = first + JOIN * (i % block)
        return (lax.broadcasted_iota(jnp.int32, (count, rows), 1) == source).astype(BF16)

    copies[5].wait()
    copies[6].wait()
    wo = wo_ref[...]
    heads = hf[...]
    def summed(section):
        chosen = jnp.dot(picked(section, 0, rows // 2), heads, preferred_element_type=F32).astype(BF16)
        return jnp.dot(chosen, wo, preferred_element_type=F32).astype(BF16)

    other = summed(1 - c)
    for zz, out in enumerate(sends):
        out[...] = other[zz * block:(zz + 1) * block, :]
    keep_ref[...] = summed(c)
    own = jnp.dot(picked(c, z, block), x_ref[...], preferred_element_type=F32)
    base_ref[...] = own + ob_ref[...][None, :]
    for copy in copies[7:]:
        copy.wait()


def pair_rows_kernel(n_z, block, keep_ref, *refs):
    z = lax.axis_index("mp")
    gots, outs = refs[:n_z], refs[n_z:]
    for k in range(n_z):
        mine = lax.rem(z + k, n_z)
        keep = keep_ref[pl.ds(pl.multiple_of(mine * block, block), block), :].astype(F32)
        for zz in range(n_z):

            @pl.when(mine == zz)
            def _():
                outs[k][...] = (keep + gots[zz][...].astype(F32)).astype(outs[k].dtype)


def resid_kernel(base_ref, gain_ref, own_ref, *refs):
    out_ref = refs[-1]
    total = own_ref[...]
    for r in refs[:-1]:
        total += r[...].astype(F32)
    x = base_ref[...] + total
    scale = lax.rsqrt(jnp.mean(x * x, axis=-1, keepdims=True) + NORM_EPS)
    out_ref[...] = (x * scale * gain_ref[...][None, :]).astype(BF16)


def hidden_kernel(n_z, block, up_ref, ub_ref, *refs):
    c, z = lax.axis_index("section"), lax.axis_index("mp")
    pieces, (out_ref, xs) = refs[:2 * n_z], refs[2 * n_z:]
    width = xs.shape[2]
    for side in range(2):
        section = c if side == 0 else 1 - c
        for k in range(n_z):
            zz = origin(z, k, n_z)
            chunk = chunk_of(section, zz, n_z)
            at = pl.ds(pl.multiple_of(chunk * block, block), block)
            xs[lax.rem(zz, JOIN), at, :] = pieces[side * n_z + k][...]
    acc = ub_ref[...][None, :]
    for q in range(JOIN):
        acc = acc + lax.dot_general(
            xs[q], up_ref[:, q * width:(q + 1) * width], NT, preferred_element_type=F32)
    out_ref[...] = (0.5 * acc * (1.0 + lax.erf(acc * (1.0 / math.sqrt(2.0))))).astype(BF16)


def down_kernel(other, hidden_ref, down_ref, *outs):
    c = lax.axis_index("section")
    width = outs[0].shape[1]
    first = (1 - c if other else c) * len(outs) * width
    for i, out in enumerate(outs):
        at = pl.ds(pl.multiple_of(first + i * width, width), width)
        out[...] = jnp.dot(hidden_ref[...], down_ref[:, at], preferred_element_type=F32).astype(BF16)


def pair_columns_kernel(n_z, *refs):
    z = lax.axis_index("mp")
    keeps, gots, outs = refs[:n_z], refs[n_z:2 * n_z], refs[2 * n_z:]
    for k in range(n_z):
        mine = lax.rem(z + k, n_z)
        for zz in range(n_z):

            @pl.when(mine == zz)
            def _():
                total = keeps[zz][...].astype(F32) + gots[zz][...].astype(F32)
                outs[k][...] = total.astype(outs[k].dtype)


def image_kernel(n_z, bias_ref, own_ref, *refs):
    out_ref = refs[-1]
    block = out_ref.shape[1]
    d = lax.axis_index("section") * n_z + lax.axis_index("mp")
    total = own_ref[...]
    for r in refs[:-1]:
        total += r[...].astype(F32)
    at = pl.ds(pl.multiple_of(d * block, block), block)
    out_ref[...] = (total + bias_ref[at][None, :]).astype(BF16)


def image_part_kernel(n_z, which, gain_ref, w_ref, *refs):
    c, z = lax.axis_index("section"), lax.axis_index("mp")
    pieces, (acc_ref, squares_ref) = refs[:-2], refs[-2:]
    rows, block = pieces[0].shape
    acc = jnp.zeros(acc_ref.shape, F32)
    squares = jnp.zeros((rows, 1), F32)
    for (side, k), piece in zip(which, pieces):
        d = (c if side == 0 else 1 - c) * n_z + origin(z, k, n_z)
        at = pl.ds(pl.multiple_of(d * block, block), block)
        x = piece[...].astype(F32)
        squares += jnp.sum(x * x, axis=-1, keepdims=True)
        acc += jnp.dot((x * gain_ref[at][None, :]).astype(BF16), w_ref[at, :], preferred_element_type=F32)
    acc_ref[...] = acc
    squares_ref[...] = jnp.broadcast_to(squares, squares_ref.shape)


def image_keyval_kernel(n_z, which, gain_ref, w_ref, b_ref, acc_ref, squares_ref, *refs):
    pieces, (out_ref, acc, squares) = refs[:-3], refs[-3:]
    image_part_kernel(n_z, which, gain_ref, w_ref, *pieces, acc, squares)
    total = squares[:, :1] + squares_ref[:, :1]
    scale = lax.rsqrt(total * (1.0 / w_ref.shape[0]) + NORM_EPS)
    out_ref[...] = ((acc[...] + acc_ref[...]) * scale + b_ref[...][None, :]).astype(BF16)


def relay_kernel(n_z, linear, *refs):
    z = lax.axis_index("mp")
    pieces, out_ref = refs[:-1], refs[-1]
    if not linear:
        for k, piece in enumerate(pieces):
            out_ref[lax.rem(z - k + n_z, n_z)] = piece[...]
        return
    pair = 1 - 2 * lax.rem(z, 2)
    far = lax.rem(z + 2, n_z)
    for at, piece in zip((z, z + pair, far, far + pair), pieces):
        out_ref[at] = piece[...]


def text_keyval_kernel(gain_ref, w_ref, b_ref, here_ref, there_ref, out_ref):
    c = lax.axis_index("section")
    blocks, rows, model = here_ref.shape
    half = blocks * rows
    acc = jnp.zeros(out_ref.shape, F32)
    squares = jnp.zeros((out_ref.shape[0], 1), F32)
    step = 1024
    for first in range(0, model, step):
        at = slice(first, first + step)
        x = jnp.concatenate([r[i, :, at] for r in (here_ref, there_ref) for i in range(blocks)], axis=0).astype(F32)
        squares += jnp.sum(x * x, axis=-1, keepdims=True)
        y = (x * gain_ref[at][None, :]).astype(BF16)
        acc += jnp.dot(y, w_ref[at, :], preferred_element_type=F32)
    scale = lax.rsqrt(squares * (1.0 / model) + NORM_EPS)
    acc = (acc * scale + b_ref[...][None, :]).astype(BF16)
    out_ref[pl.ds(pl.multiple_of(c * half, half), half), :] = acc[:half]
    out_ref[pl.ds(pl.multiple_of((1 - c) * half, half), half), :] = acc[half:]


def text_place_kernel(n_s, slot_map, place_ref, *refs):
    s = lax.axis_index("seq")
    keyvals, (out_ref, pick_ref, held) = refs[:n_s], refs[n_s:]
    units = place_ref.shape[2]
    group, width = n_s * units, pick_ref.shape[1]
    for k in range(n_s):
        held[lax.rem(s - k + n_s, n_s)] = keyvals[k][...]
    position = lax.broadcasted_iota(jnp.int32, (CTX, units), 0)
    unit = lax.broadcasted_iota(jnp.int32, (units, width), 0)
    lane = lax.broadcasted_iota(jnp.int32, (units, width), 1)

    def source(t):
        def look(n, found):
            return jnp.where(slot_map[n // n_s, n % n_s] == s * n_s + t, n, found)

        found = lax.fori_loop(0, n_s * n_s, look, 0, unroll=n_s == 4)
        return found // n_s, found % n_s

    for t in range(n_s):
        j, i = source(t)
        rows = slice(t * CTX, (t + 1) * CTX)
        chosen = (position == place_ref[i, pl.ds(j, 1), :]).astype(F32)
        covered = jnp.sum(chosen, axis=1, keepdims=True) > 0.5
        text = held[j, pl.ds(pl.multiple_of(i * CTX, CTX), CTX), :]
        out_ref[rows, :] = jnp.where(covered, 0.0, text.astype(F32))
        shift = lax.rem(s - i + n_s, n_s)
        spot = (lane == shift * group + j * units + unit).astype(BF16)
        pick_ref[rows, :] = jnp.dot(chosen.astype(BF16), spot, preferred_element_type=F32).astype(BF16)


def place_kernel(text_ref, pick_ref, *refs):
    keyvals, out_ref = refs[:-1], refs[-1]
    rows = jnp.concatenate([r[...] for r in keyvals], axis=0)
    total = text_ref[...] + jnp.dot(pick_ref[...], rows, preferred_element_type=F32)
    out_ref[...] = total.astype(BF16).reshape(out_ref.shape)


def shards(
    patches,
    image_place,
    slot_map,
    text,
    vision_gain,
    qkv_weight,
    qkv_bias,
    out_weight,
    out_bias,
    merge_gain,
    merge_up,
    merge_up_bias,
    merge_down,
    merge_down_bias,
    input_gain,
    kv_weight,
    kv_bias,
):
    n_z, n_s = lax.axis_size("mp"), lax.axis_size("seq")
    n_d = lax.axis_size("section") * n_z
    x = patches[0]
    rows, width = x.shape
    units = rows // JOIN
    block = rows // n_d
    head_width = out_weight.shape[0]
    model = merge_down.shape[1]
    columns = model // n_d
    kv_width = kv_weight.shape[1]

    def swap(v):
        return lax.ppermute(v, "section", [(0, 1), (1, 0)])

    linear = n_z == 4

    def near(v):
        return lax.ppermute(v, "mp", [(0, 1), (1, 0), (2, 3), (3, 2)])

    def across(v):
        return lax.ppermute(v, "mp", [(0, 2), (2, 0), (1, 3), (3, 1)])

    def spread(own):
        here = [own] + [shifted(own, "mp", n_z, k) for k in range(1, n_z)]
        return here + [swap(v) for v in here]

    text_own = text[0]

    if linear:
        across_own, near_own = across(text_own), near(text_own)
        near_across = near(across_own)
        text_pieces = [text_own, near_own, across_own, near_across]
        early, late = [across_own, near_own], [near_across]
    else:
        text_pieces = [text_own] + [shifted(text_own, "mp", n_z, k) for k in range(1, n_z)]
        early, late = text_pieces[1:2], text_pieces[2:3]

    w = qkv_weight.transpose(1, 2, 0).reshape(3 * head_width, width)
    later = [merge_gain, merge_up.T, merge_up_bias, merge_down_bias, input_gain, kv_bias]
    keep, base, *rest = call(
        functools.partial(front_kernel, n_z, block, len(later)),
        [struct((rows // 2, width), BF16), struct((block, width), F32)]
        + [struct((block, width), BF16)] * n_z
        + [struct(v.shape, v.dtype) for v in later],
        [image_place, x, vision_gain, w, qkv_bias, out_weight, out_bias] + later,
        scratch=[
            pltpu.VMEM((rows, head_width), BF16), pltpu.SMEM(image_place.shape, jnp.int32),
            pltpu.VMEM(x.shape, BF16), pltpu.VMEM(vision_gain.shape, F32), pltpu.VMEM(w.shape, BF16),
            pltpu.VMEM(qkv_bias.shape, F32), pltpu.VMEM(out_weight.shape, BF16), pltpu.VMEM(out_bias.shape, F32),
            pltpu.SemaphoreType.DMA((7 + len(later),)),
        ],
        raw=True,
        grant=24,
        flops=2 * rows * width * 4 * head_width,
    )
    sends, (gain, up, up_bias, down_bias, text_gain, bias) = rest[:n_z], rest[n_z:]
    parts = call(
        functools.partial(pair_rows_kernel, n_z, block),
        [struct((block, width), F32)] + [struct((block, width), BF16)] * (n_z - 1),
        [keep] + [swap(v) for v in sends],
    )
    sums = [parts[0]] + [shifted(parts[k], "mp", n_z, k) for k in range(1, n_z)]
    merged, = call(
        resid_kernel, [struct((block, width), BF16)], [base, gain] + sums, after=early)
    pieces = spread(merged)

    hidden, = call(
        functools.partial(hidden_kernel, n_z, block),
        [struct((units, merge_up.shape[1]), BF16)],
        [up, up_bias] + pieces,
        scratch=[pltpu.VMEM((JOIN, units, width), BF16)],
        flops=2 * units * merge_up.size,
    )
    sends, keeps = (
        call(
            functools.partial(down_kernel, other),
            [struct((units, columns), BF16)] * n_z,
            [hidden, merge_down],
            after=late if other else (),
            flops=units * merge_down.size,
            grant=16,
        )
        for other in (True, False)
    )
    parts = call(
        functools.partial(pair_columns_kernel, n_z),
        [struct((units, columns), F32)] + [struct((units, columns), BF16)] * (n_z - 1),
        [*keeps, *(swap(v) for v in sends)],
    )
    sums = [parts[0]] + [shifted(parts[k], "mp", n_z, k) for k in range(1, n_z)]
    line, = call(
        functools.partial(relay_kernel, n_z, linear), [struct((n_z,) + text_own.shape, BF16)], text_pieces, after=parts[:1])
    prompt = n_d * text.shape[1]
    text_keyval, = call(
        text_keyval_kernel,
        [struct((prompt, kv_width), BF16)],
        [text_gain, kv_weight, bias, line, swap(line)],
        flops=2 * prompt * model * kv_width,
        grant=16,
    )
    texts = [text_keyval] + [shifted(text_keyval, "seq", n_s, k) for k in range(1, n_s)]
    image, = call(
        functools.partial(image_kernel, n_z), [struct((units, columns), BF16)], [down_bias] + sums, after=texts[1:])
    image_pieces = spread(image)

    text_placed, pick = call(
        functools.partial(text_place_kernel, n_s),
        [struct((n_s * CTX, kv_width), F32), struct((n_s * CTX, n_s * units), BF16)],
        [slot_map, image_place] + texts,
        scratch=[pltpu.VMEM((n_s, prompt, kv_width), BF16)],
        smem=1,
        grant=24,
    )

    sides = [(i // n_z, i % n_z) for i in range(2 * n_z)]
    first, last = ([s for s in sides if (s[1] == n_z - 1) == end] for end in (False, True))
    acc, squares = call(
        functools.partial(image_part_kernel, n_z, first),
        [struct((units, kv_width), F32), struct((units, 128), F32)],
        [text_gain, kv_weight] + [image_pieces[side * n_z + k] for side, k in first],
        flops=units * model * kv_width,
        grant=16,
    )
    keyval, = call(
        functools.partial(image_keyval_kernel, n_z, last),
        [struct((units, kv_width), BF16)],
        [text_gain, kv_weight, bias, acc, squares] + [image_pieces[side * n_z + k] for side, k in last],
        scratch=[pltpu.VMEM((units, kv_width), F32), pltpu.VMEM((units, 128), F32)],
        grant=16,
    )
    keyvals = [keyval] + [shifted(keyval, "seq", n_s, k) for k in range(1, n_s)]
    cache, = call(
        place_kernel, [struct((n_s, CTX, kv_width), BF16)], [text_placed, pick] + keyvals, grant=24)
    return cache[None]


def solution(mesh):
    placed = (
        P("seq", None, None),
        P(),
        P(),
        P("seq", ("section", "mp"), None),
        P(),
        P(None, None, ("section", "mp")),
        P(None, ("section", "mp")),
        P(("section", "mp"), None),
        P(),
        P(),
        P(None, ("section", "mp")),
        P(("section", "mp")),
        P(("section", "mp"), None),
        P(),
        P(),
        P(None, ("section", "mp")),
        P(("section", "mp")),
    )
    return jax.shard_map(
        shards,
        mesh=mesh,
        in_specs=placed,
        out_specs=P("section", "seq", None, "mp"),
        check_vma=False,
    )
```

```python
import functools
import math

import jax
import jax.numpy as jnp
from jax import lax
from jax.experimental import pallas as pl
from jax.experimental.pallas import tpu as pltpu
from jax.sharding import PartitionSpec as P

VHEAD = 80
CTX = 32
WIN = 64
JOIN = 4
NORM_EPS = 1e-06
F32 = jnp.float32
BF16 = jnp.bfloat16
MIB = 1024 * 1024
NT = (((1,), (1,)), ((), ()))


def call(kernel, outs, args, after=(), scratch=(), smem=0, raw=False, flops=0, grant=8):
    space = pl.BlockSpec(memory_space=pltpu.HBM if raw else pltpu.VMEM)
    scalar = pl.BlockSpec(memory_space=pltpu.SMEM)
    unread = pl.BlockSpec(memory_space=pl.ANY)
    moved = sum(math.prod(a.shape) * a.dtype.itemsize for a in list(args) + list(outs))
    count = len(after)
    if raw:
        args = [pltpu.with_memory_space_constraint(a, pltpu.HBM) for a in args]

    def body(*refs):
        kernel(*refs[count:])

    return pl.pallas_call(
        body,
        out_shape=outs,
        in_specs=[unread] * count + [scalar] * smem + [space] * (len(args) - smem),
        out_specs=[pl.BlockSpec(memory_space=pltpu.VMEM)] * len(outs),
        scratch_shapes=list(scratch),
        compiler_params=pltpu.CompilerParams(vmem_limit_bytes=grant * MIB),
        cost_estimate=pl.CostEstimate(flops=flops, bytes_accessed=moved, transcendentals=0),
    )(*after, *args)


def struct(shape, dtype):
    return jax.ShapeDtypeStruct(shape, dtype)


def shifted(x, axis, count, k):
    return lax.ppermute(x, axis, [(i, (i + k) % count) for i in range(count)])


def origin(z, k, n_z, hops):
    return lax.bitwise_xor(z, jnp.int32(k)) if hops and n_z == 4 else lax.rem(z - k + n_z, n_z)


def chunk_of(section, z, n_z):
    return section * (n_z // JOIN) + z // JOIN


def front_kernel(n_z, block, kept, place_hbm, x_hbm, gain_hbm, w_hbm, b_hbm, wo_hbm, ob_hbm, *refs):
    later, refs = refs[:kept], refs[kept:]
    (keep_ref, base_ref), sends, refs = refs[:2], refs[2:2 + n_z], refs[2 + n_z:]
    held, refs = refs[:kept], refs[kept:]
    hf, place, x_ref, gain_ref, w_ref, b_ref, wo_ref, ob_ref, sems = refs
    brought = (
        (x_hbm, x_ref), (gain_hbm, gain_ref), (w_hbm, w_ref), (b_hbm, b_ref),
        (place_hbm, place), (wo_hbm, wo_ref), (ob_hbm, ob_ref), *zip(later, held),
    )
    copies = [pltpu.make_async_copy(a, b, sems.at[i]) for i, (a, b) in enumerate(brought)]
    for copy in copies:
        copy.start()
    c, z, s = lax.axis_index("section"), lax.axis_index("mp"), lax.axis_index("seq")
    rows, width = x_ref.shape
    head_width = hf.shape[1]
    units = place.shape[2]
    tile = 256
    per_tile = tile // WIN
    for copy in copies[:5]:
        copy.wait()

    def one(t, carry):
        at = pl.ds(pl.multiple_of(t * tile, tile), tile)
        x = x_ref[at, :].astype(F32)
        scale = lax.rsqrt(jnp.mean(x * x, axis=-1, keepdims=True) + NORM_EPS)
        y = (x * scale * gain_ref[...][None, :]).astype(BF16)
        parts = []
        for i in range(3):
            w = w_ref[i * head_width:(i + 1) * head_width, :]
            part = lax.dot_general(y, w, NT, preferred_element_type=F32)
            parts.append((part + b_ref[i:i + 1, :]).astype(BF16))
        q, k, v = parts
        key = lax.broadcasted_iota(jnp.int32, (tile, tile), 1)
        row = lax.broadcasted_iota(jnp.int32, (tile, tile), 0)
        same = key // WIN == row // WIN
        end = jnp.zeros((tile, tile), jnp.int32)
        for j in range(per_tile):
            count = jnp.int32(0)
            for u in range(units):
                count += (place[s, t * per_tile + j, u] >= 0).astype(jnp.int32)
            end = jnp.where(key // WIN == j, j * WIN + count * JOIN, end)
        live = same & (key < end)
        lane = lax.broadcasted_iota(jnp.int32, (1, head_width), 1)
        total = jnp.zeros((tile, head_width), F32)
        for h in range(head_width // VHEAD):
            mine = lane // VHEAD == h
            qh = jnp.where(mine, q, jnp.zeros_like(q))
            scores = lax.dot_general(qh, k, NT, preferred_element_type=F32) * (1.0 / math.sqrt(VHEAD))
            raised = jnp.where(live, jnp.exp(scores), 0.0)
            probs = (raised / jnp.sum(raised, axis=-1, keepdims=True)).astype(BF16)
            out = jnp.dot(probs, v, preferred_element_type=F32)
            total = jnp.where(mine, out, total)
        hf[at, :] = total.astype(BF16)
        return carry

    if rows == tile:
        one(0, 0)
    else:
        lax.fori_loop(0, rows // tile, one, 0)

    def picked(section, zz, count):
        i = lax.broadcasted_iota(jnp.int32, (count, rows), 0)
        device = zz + i // block
        first = JOIN * block * chunk_of(section, device, n_z) + device % JOIN
        source = first + JOIN * (i % block)
        return (lax.broadcasted_iota(jnp.int32, (count, rows), 1) == source).astype(BF16)

    copies[5].wait()
    copies[6].wait()
    wo = wo_ref[...]
    heads = hf[...]
    def summed(section):
        chosen = jnp.dot(picked(section, 0, rows // 2), heads, preferred_element_type=F32).astype(BF16)
        return jnp.dot(chosen, wo, preferred_element_type=F32).astype(BF16)

    other = summed(1 - c)
    for zz, out in enumerate(sends):
        out[...] = other[zz * block:(zz + 1) * block, :]
    keep_ref[...] = summed(c)
    own = jnp.dot(picked(c, z, block), x_ref[...], preferred_element_type=F32)
    base_ref[...] = own + ob_ref[...][None, :]
    for copy in copies[7:]:
        copy.wait()


def pair_rows_kernel(n_z, block, keep_ref, *refs):
    z = lax.axis_index("mp")
    gots, outs = refs[:n_z], refs[n_z:]
    for k in range(n_z):
        mine = lax.rem(z + k, n_z)
        keep = keep_ref[pl.ds(pl.multiple_of(mine * block, block), block), :].astype(F32)
        for zz in range(n_z):

            @pl.when(mine == zz)
            def _():
                outs[k][...] = (keep + gots[zz][...].astype(F32)).astype(outs[k].dtype)


def resid_kernel(base_ref, gain_ref, own_ref, *refs):
    out_ref = refs[-1]
    total = own_ref[...]
    for r in refs[:-1]:
        total += r[...].astype(F32)
    x = base_ref[...] + total
    scale = lax.rsqrt(jnp.mean(x * x, axis=-1, keepdims=True) + NORM_EPS)
    out_ref[...] = (x * scale * gain_ref[...][None, :]).astype(BF16)


def hidden_kernel(n_z, block, up_ref, ub_ref, *refs):
    c, z = lax.axis_index("section"), lax.axis_index("mp")
    pieces, (out_ref, xs) = refs[:2 * n_z], refs[2 * n_z:]
    width = xs.shape[2]
    for side in range(2):
        section = c if side == 0 else 1 - c
        for k in range(n_z):
            zz = origin(z, k, n_z, False)
            chunk = chunk_of(section, zz, n_z)
            at = pl.ds(pl.multiple_of(chunk * block, block), block)
            xs[lax.rem(zz, JOIN), at, :] = pieces[side * n_z + k][...]
    acc = ub_ref[...][None, :]
    for q in range(JOIN):
        acc = acc + lax.dot_general(
            xs[q], up_ref[:, q * width:(q + 1) * width], NT, preferred_element_type=F32)
    out_ref[...] = (0.5 * acc * (1.0 + lax.erf(acc * (1.0 / math.sqrt(2.0))))).astype(BF16)


def down_kernel(other, hidden_ref, down_ref, *outs):
    c = lax.axis_index("section")
    width = outs[0].shape[1]
    first = (1 - c if other else c) * len(outs) * width
    for i, out in enumerate(outs):
        at = pl.ds(pl.multiple_of(first + i * width, width), width)
        out[...] = jnp.dot(hidden_ref[...], down_ref[:, at], preferred_element_type=F32).astype(BF16)


def pair_columns_kernel(n_z, *refs):
    z = lax.axis_index("mp")
    keeps, gots, outs = refs[:n_z], refs[n_z:2 * n_z], refs[2 * n_z:]
    for k in range(n_z):
        mine = lax.rem(z + k, n_z)
        for zz in range(n_z):

            @pl.when(mine == zz)
            def _():
                total = keeps[zz][...].astype(F32) + gots[zz][...].astype(F32)
                outs[k][...] = total.astype(outs[k].dtype)


def image_kernel(n_z, bias_ref, own_ref, *refs):
    out_ref = refs[-1]
    block = out_ref.shape[1]
    d = lax.axis_index("section") * n_z + lax.axis_index("mp")
    total = own_ref[...]
    for r in refs[:-1]:
        total += r[...].astype(F32)
    at = pl.ds(pl.multiple_of(d * block, block), block)
    out_ref[...] = (total + bias_ref[at][None, :]).astype(BF16)


def image_part_kernel(n_z, which, gain_ref, w_ref, *refs):
    c, z = lax.axis_index("section"), lax.axis_index("mp")
    pieces, (acc_ref, squares_ref) = refs[:-2], refs[-2:]
    rows, block = pieces[0].shape
    acc = jnp.zeros(acc_ref.shape, F32)
    squares = jnp.zeros((rows, 1), F32)
    for (side, k), piece in zip(which, pieces):
        d = (c if side == 0 else 1 - c) * n_z + origin(z, k, n_z, True)
        at = pl.ds(pl.multiple_of(d * block, block), block)
        x = piece[...].astype(F32)
        squares += jnp.sum(x * x, axis=-1, keepdims=True)
        acc += jnp.dot((x * gain_ref[at][None, :]).astype(BF16), w_ref[at, :], preferred_element_type=F32)
    acc_ref[...] = acc
    squares_ref[...] = jnp.broadcast_to(squares, squares_ref.shape)


def image_keyval_kernel(n_z, which, gain_ref, w_ref, b_ref, acc_ref, squares_ref, *refs):
    pieces, (out_ref, acc, squares) = refs[:-3], refs[-3:]
    image_part_kernel(n_z, which, gain_ref, w_ref, *pieces, acc, squares)
    total = squares[:, :1] + squares_ref[:, :1]
    scale = lax.rsqrt(total * (1.0 / w_ref.shape[0]) + NORM_EPS)
    out_ref[...] = ((acc[...] + acc_ref[...]) * scale + b_ref[...][None, :]).astype(BF16)


def relay_kernel(n_z, linear, *refs):
    z = lax.axis_index("mp")
    pieces, out_ref = refs[:-1], refs[-1]
    if not linear:
        for k, piece in enumerate(pieces):
            out_ref[lax.rem(z - k + n_z, n_z)] = piece[...]
        return
    pair = 1 - 2 * lax.rem(z, 2)
    far = lax.rem(z + 2, n_z)
    for at, piece in zip((z, z + pair, far, far + pair), pieces):
        out_ref[at] = piece[...]


def text_keyval_kernel(gain_ref, w_ref, b_ref, here_ref, there_ref, out_ref):
    c = lax.axis_index("section")
    blocks, rows, model = here_ref.shape
    half = blocks * rows
    acc = jnp.zeros(out_ref.shape, F32)
    squares = jnp.zeros((out_ref.shape[0], 1), F32)
    step = 1024
    for first in range(0, model, step):
        at = slice(first, first + step)
        x = jnp.concatenate([r[i, :, at] for r in (here_ref, there_ref) for i in range(blocks)], axis=0).astype(F32)
        squares += jnp.sum(x * x, axis=-1, keepdims=True)
        y = (x * gain_ref[at][None, :]).astype(BF16)
        acc += jnp.dot(y, w_ref[at, :], preferred_element_type=F32)
    scale = lax.rsqrt(squares * (1.0 / model) + NORM_EPS)
    acc = (acc * scale + b_ref[...][None, :]).astype(BF16)
    out_ref[pl.ds(pl.multiple_of(c * half, half), half), :] = acc[:half]
    out_ref[pl.ds(pl.multiple_of((1 - c) * half, half), half), :] = acc[half:]


def text_place_kernel(n_s, slot_map, place_ref, *refs):
    s = lax.axis_index("seq")
    keyvals, (out_ref, pick_ref, held) = refs[:n_s], refs[n_s:]
    units = place_ref.shape[2]
    group, width = n_s * units, pick_ref.shape[1]
    for k in range(n_s):
        held[lax.rem(s - k + n_s, n_s)] = keyvals[k][...]
    position = lax.broadcasted_iota(jnp.int32, (CTX, units), 0)
    unit = lax.broadcasted_iota(jnp.int32, (units, width), 0)
    lane = lax.broadcasted_iota(jnp.int32, (units, width), 1)

    def source(t):
        def look(n, found):
            return jnp.where(slot_map[n // n_s, n % n_s] == s * n_s + t, n, found)

        found = lax.fori_loop(0, n_s * n_s, look, 0, unroll=n_s == 4)
        return found // n_s, found % n_s

    for t in range(n_s):
        j, i = source(t)
        rows = slice(t * CTX, (t + 1) * CTX)
        chosen = (position == place_ref[i, pl.ds(j, 1), :]).astype(F32)
        covered = jnp.sum(chosen, axis=1, keepdims=True) > 0.5
        text = held[j, pl.ds(pl.multiple_of(i * CTX, CTX), CTX), :]
        out_ref[rows, :] = jnp.where(covered, 0.0, text.astype(F32))
        shift = lax.rem(s - i + n_s, n_s)
        spot = (lane == shift * group + j * units + unit).astype(BF16)
        pick_ref[rows, :] = jnp.dot(chosen.astype(BF16), spot, preferred_element_type=F32).astype(BF16)


def place_kernel(text_ref, pick_ref, *refs):
    keyvals, out_ref = refs[:-1], refs[-1]
    rows = jnp.concatenate([r[...] for r in keyvals], axis=0)
    total = text_ref[...] + jnp.dot(pick_ref[...], rows, preferred_element_type=F32)
    out_ref[...] = total.astype(BF16).reshape(out_ref.shape)


def shards(
    patches,
    image_place,
    slot_map,
    text,
    vision_gain,
    qkv_weight,
    qkv_bias,
    out_weight,
    out_bias,
    merge_gain,
    merge_up,
    merge_up_bias,
    merge_down,
    merge_down_bias,
    input_gain,
    kv_weight,
    kv_bias,
):
    n_z, n_s = lax.axis_size("mp"), lax.axis_size("seq")
    n_d = lax.axis_size("section") * n_z
    x = patches[0]
    rows, width = x.shape
    units = rows // JOIN
    block = rows // n_d
    head_width = out_weight.shape[0]
    model = merge_down.shape[1]
    columns = model // n_d
    kv_width = kv_weight.shape[1]

    def swap(v):
        return lax.ppermute(v, "section", [(0, 1), (1, 0)])

    linear = n_z == 4

    def near(v):
        return lax.ppermute(v, "mp", [(0, 1), (1, 0), (2, 3), (3, 2)])

    def across(v):
        return lax.ppermute(v, "mp", [(0, 2), (2, 0), (1, 3), (3, 1)])

    def spread(own, hops):
        if linear and hops:
            far, beside = across(own), near(own)
            here = [own, beside, far]
            swapped = [swap(v) for v in here]
            last = near(far)
            return here + [last] + swapped + [swap(last)]
        else:
            here = [own] + [shifted(own, "mp", n_z, k) for k in range(1, n_z)]
        return here + [swap(v) for v in here]

    text_own = text[0]

    if linear:
        across_own, near_own = across(text_own), near(text_own)
        near_across = near(across_own)
        text_pieces = [text_own, near_own, across_own, near_across]
        early, late = [across_own, near_own], [near_across]
    else:
        text_pieces = [text_own] + [shifted(text_own, "mp", n_z, k) for k in range(1, n_z)]
        early, late = text_pieces[1:2], text_pieces[2:3]

    w = qkv_weight.transpose(1, 2, 0).reshape(3 * head_width, width)
    later = [merge_gain, merge_up.T, merge_up_bias, merge_down_bias, input_gain, kv_bias]
    keep, base, *rest = call(
        functools.partial(front_kernel, n_z, block, len(later)),
        [struct((rows // 2, width), BF16), struct((block, width), F32)]
        + [struct((block, width), BF16)] * n_z
        + [struct(v.shape, v.dtype) for v in later],
        [image_place, x, vision_gain, w, qkv_bias, out_weight, out_bias] + later,
        scratch=[
            pltpu.VMEM((rows, head_width), BF16), pltpu.SMEM(image_place.shape, jnp.int32),
            pltpu.VMEM(x.shape, BF16), pltpu.VMEM(vision_gain.shape, F32), pltpu.VMEM(w.shape, BF16),
            pltpu.VMEM(qkv_bias.shape, F32), pltpu.VMEM(out_weight.shape, BF16), pltpu.VMEM(out_bias.shape, F32),
            pltpu.SemaphoreType.DMA((7 + len(later),)),
        ],
        raw=True,
        grant=24,
        flops=2 * rows * width * 4 * head_width,
    )
    sends, (gain, up, up_bias, down_bias, text_gain, bias) = rest[:n_z], rest[n_z:]
    parts = call(
        functools.partial(pair_rows_kernel, n_z, block),
        [struct((block, width), F32)] + [struct((block, width), BF16)] * (n_z - 1),
        [keep] + [swap(v) for v in sends],
    )
    sums = [parts[0]] + [shifted(parts[k], "mp", n_z, k) for k in range(1, n_z)]
    merged, = call(
        resid_kernel, [struct((block, width), BF16)], [base, gain] + sums, after=early)
    pieces = spread(merged, False)

    hidden, = call(
        functools.partial(hidden_kernel, n_z, block),
        [struct((units, merge_up.shape[1]), BF16)],
        [up, up_bias] + pieces,
        scratch=[pltpu.VMEM((JOIN, units, width), BF16)],
        flops=2 * units * merge_up.size,
    )
    sends, keeps = (
        call(
            functools.partial(down_kernel, other),
            [struct((units, columns), BF16)] * n_z,
            [hidden, merge_down],
            after=late if other else (),
            flops=units * merge_down.size,
            grant=16,
        )
        for other in (True, False)
    )
    parts = call(
        functools.partial(pair_columns_kernel, n_z),
        [struct((units, columns), F32)] + [struct((units, columns), BF16)] * (n_z - 1),
        [*keeps, *(swap(v) for v in sends)],
    )
    sums = [parts[0]] + [shifted(parts[k], "mp", n_z, k) for k in range(1, n_z)]
    line, = call(
        functools.partial(relay_kernel, n_z, linear), [struct((n_z,) + text_own.shape, BF16)], text_pieces, after=parts[:1])
    prompt = n_d * text.shape[1]
    text_keyval, = call(
        text_keyval_kernel,
        [struct((prompt, kv_width), BF16)],
        [text_gain, kv_weight, bias, line, swap(line)],
        flops=2 * prompt * model * kv_width,
        grant=16,
    )
    texts = [text_keyval] + [shifted(text_keyval, "seq", n_s, k) for k in range(1, n_s)]
    image, = call(
        functools.partial(image_kernel, n_z), [struct((units, columns), BF16)], [down_bias] + sums, after=texts[1:])
    image_pieces = spread(image, True)

    text_placed, pick = call(
        functools.partial(text_place_kernel, n_s),
        [struct((n_s * CTX, kv_width), F32), struct((n_s * CTX, n_s * units), BF16)],
        [slot_map, image_place] + texts,
        scratch=[pltpu.VMEM((n_s, prompt, kv_width), BF16)],
        smem=1,
        grant=24,
    )

    sides = [(i // n_z, i % n_z) for i in range(2 * n_z)]
    first, last = ([s for s in sides if (s[1] == n_z - 1) == end] for end in (False, True))
    acc, squares = call(
        functools.partial(image_part_kernel, n_z, first),
        [struct((units, kv_width), F32), struct((units, 128), F32)],
        [text_gain, kv_weight] + [image_pieces[side * n_z + k] for side, k in first],
        flops=units * model * kv_width,
        grant=16,
    )
    keyval, = call(
        functools.partial(image_keyval_kernel, n_z, last),
        [struct((units, kv_width), BF16)],
        [text_gain, kv_weight, bias, acc, squares] + [image_pieces[side * n_z + k] for side, k in last],
        scratch=[pltpu.VMEM((units, kv_width), F32), pltpu.VMEM((units, 128), F32)],
        grant=16,
    )
    keyvals = [keyval] + [shifted(keyval, "seq", n_s, k) for k in range(1, n_s)]
    cache, = call(
        place_kernel, [struct((n_s, CTX, kv_width), BF16)], [text_placed, pick] + keyvals, grant=24)
    return cache[None]


def solution(mesh):
    placed = (
        P("seq", None, None),
        P(),
        P(),
        P("seq", ("section", "mp"), None),
        P(),
        P(None, None, ("section", "mp")),
        P(None, ("section", "mp")),
        P(("section", "mp"), None),
        P(),
        P(),
        P(None, ("section", "mp")),
        P(("section", "mp")),
        P(("section", "mp"), None),
        P(),
        P(),
        P(None, ("section", "mp")),
        P(("section", "mp")),
    )
    return jax.shard_map(
        shards,
        mesh=mesh,
        in_specs=placed,
        out_specs=P("section", "seq", None, "mp"),
        check_vma=False,
    )
```

```python
import functools
import math

import jax
import jax.numpy as jnp
from jax import lax
from jax.experimental import pallas as pl
from jax.experimental.pallas import tpu as pltpu
from jax.sharding import PartitionSpec as P

VHEAD = 80
CTX = 32
WIN = 64
JOIN = 4
NORM_EPS = 1e-06
F32 = jnp.float32
BF16 = jnp.bfloat16
MIB = 1024 * 1024
NT = (((1,), (1,)), ((), ()))


def call(kernel, outs, args, after=(), scratch=(), smem=0, raw=False, flops=0, grant=8):
    space = pl.BlockSpec(memory_space=pltpu.HBM if raw else pltpu.VMEM)
    scalar = pl.BlockSpec(memory_space=pltpu.SMEM)
    unread = pl.BlockSpec(memory_space=pl.ANY)
    moved = sum(math.prod(a.shape) * a.dtype.itemsize for a in list(args) + list(outs))
    count = len(after)
    if raw:
        args = [pltpu.with_memory_space_constraint(a, pltpu.HBM) for a in args]

    def body(*refs):
        kernel(*refs[count:])

    return pl.pallas_call(
        body,
        out_shape=outs,
        in_specs=[unread] * count + [scalar] * smem + [space] * (len(args) - smem),
        out_specs=[pl.BlockSpec(memory_space=pltpu.VMEM)] * len(outs),
        scratch_shapes=list(scratch),
        compiler_params=pltpu.CompilerParams(vmem_limit_bytes=grant * MIB),
        cost_estimate=pl.CostEstimate(flops=flops, bytes_accessed=moved, transcendentals=0),
    )(*after, *args)


def struct(shape, dtype):
    return jax.ShapeDtypeStruct(shape, dtype)


def shifted(x, axis, count, k):
    return lax.ppermute(x, axis, [(i, (i + k) % count) for i in range(count)])


def origin(z, k, n_z):
    return lax.rem(z - k + n_z, n_z)


def chunk_of(section, z, n_z):
    return section * (n_z // JOIN) + z // JOIN


def front_kernel(n_z, block, kept, place_hbm, x_hbm, gain_hbm, w_hbm, b_hbm, wo_hbm, ob_hbm, *refs):
    later, refs = refs[:kept], refs[kept:]
    (keep_ref, base_ref), sends, refs = refs[:2], refs[2:2 + n_z], refs[2 + n_z:]
    held, refs = refs[:kept], refs[kept:]
    hf, place, x_ref, gain_ref, w_ref, b_ref, wo_ref, ob_ref, sems = refs
    brought = (
        (x_hbm, x_ref), (gain_hbm, gain_ref), (w_hbm, w_ref), (b_hbm, b_ref),
        (place_hbm, place), (wo_hbm, wo_ref), (ob_hbm, ob_ref), *zip(later, held),
    )
    copies = [pltpu.make_async_copy(a, b, sems.at[i]) for i, (a, b) in enumerate(brought)]
    for copy in copies:
        copy.start()
    c, z, s = lax.axis_index("section"), lax.axis_index("mp"), lax.axis_index("seq")
    rows, width = x_ref.shape
    head_width = hf.shape[1]
    units = place.shape[2]
    tile = 256
    per_tile = tile // WIN
    single = rows == tile

    def wait(*which, inside=True):
        if inside == single:
            for i in which:
                copies[i].wait()

    wait(0, 1, 2, 3, 4, inside=False)

    def one(t, carry):
        at = pl.ds(pl.multiple_of(t * tile, tile), tile)
        wait(0, 1)
        x = x_ref[at, :].astype(F32)
        scale = lax.rsqrt(jnp.mean(x * x, axis=-1, keepdims=True) + NORM_EPS)
        y = (x * scale * gain_ref[...][None, :]).astype(BF16)
        wait(2, 3)
        parts = []
        for i in range(3):
            w = w_ref[i * head_width:(i + 1) * head_width, :]
            part = lax.dot_general(y, w, NT, preferred_element_type=F32)
            parts.append((part + b_ref[i:i + 1, :]).astype(BF16))
        q, k, v = parts
        key = lax.broadcasted_iota(jnp.int32, (tile, tile), 1)
        row = lax.broadcasted_iota(jnp.int32, (tile, tile), 0)
        same = key // WIN == row // WIN
        wait(4)
        end = jnp.zeros((tile, tile), jnp.int32)
        for j in range(per_tile):
            count = jnp.int32(0)
            for u in range(units):
                count += (place[s, t * per_tile + j, u] >= 0).astype(jnp.int32)
            end = jnp.where(key // WIN == j, j * WIN + count * JOIN, end)
        live = same & (key < end)
        lane = lax.broadcasted_iota(jnp.int32, (1, head_width), 1)
        total = jnp.zeros((tile, head_width), F32)
        for h in range(head_width // VHEAD):
            mine = lane // VHEAD == h
            qh = jnp.where(mine, q, jnp.zeros_like(q))
            scores = lax.dot_general(qh, k, NT, preferred_element_type=F32) * (1.0 / math.sqrt(VHEAD))
            raised = jnp.where(live, jnp.exp(scores), 0.0)
            probs = (raised / jnp.sum(raised, axis=-1, keepdims=True)).astype(BF16)
            out = jnp.dot(probs, v, preferred_element_type=F32)
            total = jnp.where(mine, out, total)
        hf[at, :] = total.astype(BF16)
        return carry

    if single:
        one(0, 0)
    else:
        lax.fori_loop(0, rows // tile, one, 0)

    def picked(section, zz, count):
        i = lax.broadcasted_iota(jnp.int32, (count, rows), 0)
        device = zz + i // block
        first = JOIN * block * chunk_of(section, device, n_z) + device % JOIN
        source = first + JOIN * (i % block)
        return (lax.broadcasted_iota(jnp.int32, (count, rows), 1) == source).astype(BF16)

    copies[5].wait()
    copies[6].wait()
    wo = wo_ref[...]
    heads = hf[...]
    def summed(section):
        chosen = jnp.dot(picked(section, 0, rows // 2), heads, preferred_element_type=F32).astype(BF16)
        return jnp.dot(chosen, wo, preferred_element_type=F32).astype(BF16)

    other = summed(1 - c)
    for zz, out in enumerate(sends):
        out[...] = other[zz * block:(zz + 1) * block, :]
    keep_ref[...] = summed(c)
    own = jnp.dot(picked(c, z, block), x_ref[...], preferred_element_type=F32)
    base_ref[...] = own + ob_ref[...][None, :]
    for copy in copies[7:]:
        copy.wait()


def pair_rows_kernel(n_z, block, keep_ref, *refs):
    z = lax.axis_index("mp")
    gots, outs = refs[:n_z], refs[n_z:]
    for k in range(n_z):
        mine = lax.rem(z + k, n_z)
        keep = keep_ref[pl.ds(pl.multiple_of(mine * block, block), block), :].astype(F32)
        for zz in range(n_z):

            @pl.when(mine == zz)
            def _():
                outs[k][...] = (keep + gots[zz][...].astype(F32)).astype(outs[k].dtype)


def resid_kernel(base_ref, gain_ref, own_ref, *refs):
    out_ref = refs[-1]
    total = own_ref[...]
    for r in refs[:-1]:
        total += r[...].astype(F32)
    x = base_ref[...] + total
    scale = lax.rsqrt(jnp.mean(x * x, axis=-1, keepdims=True) + NORM_EPS)
    out_ref[...] = (x * scale * gain_ref[...][None, :]).astype(BF16)


def hidden_kernel(n_z, block, up_ref, ub_ref, *refs):
    c, z = lax.axis_index("section"), lax.axis_index("mp")
    pieces, (out_ref, xs) = refs[:2 * n_z], refs[2 * n_z:]
    width = xs.shape[2]
    for side in range(2):
        section = c if side == 0 else 1 - c
        for k in range(n_z):
            zz = origin(z, k, n_z)
            chunk = chunk_of(section, zz, n_z)
            at = pl.ds(pl.multiple_of(chunk * block, block), block)
            xs[lax.rem(zz, JOIN), at, :] = pieces[side * n_z + k][...]
    acc = ub_ref[...][None, :]
    for q in range(JOIN):
        acc = acc + lax.dot_general(
            xs[q], up_ref[:, q * width:(q + 1) * width], NT, preferred_element_type=F32)
    out_ref[...] = (0.5 * acc * (1.0 + lax.erf(acc * (1.0 / math.sqrt(2.0))))).astype(BF16)


def down_kernel(other, hidden_ref, down_ref, *outs):
    c = lax.axis_index("section")
    width = outs[0].shape[1]
    first = (1 - c if other else c) * len(outs) * width
    for i, out in enumerate(outs):
        at = pl.ds(pl.multiple_of(first + i * width, width), width)
        out[...] = jnp.dot(hidden_ref[...], down_ref[:, at], preferred_element_type=F32).astype(BF16)


def pair_columns_kernel(n_z, *refs):
    z = lax.axis_index("mp")
    keeps, gots, outs = refs[:n_z], refs[n_z:2 * n_z], refs[2 * n_z:]
    for k in range(n_z):
        mine = lax.rem(z + k, n_z)
        for zz in range(n_z):

            @pl.when(mine == zz)
            def _():
                total = keeps[zz][...].astype(F32) + gots[zz][...].astype(F32)
                outs[k][...] = total.astype(outs[k].dtype)


def image_kernel(n_z, bias_ref, own_ref, *refs):
    out_ref = refs[-1]
    block = out_ref.shape[1]
    d = lax.axis_index("section") * n_z + lax.axis_index("mp")
    total = own_ref[...]
    for r in refs[:-1]:
        total += r[...].astype(F32)
    at = pl.ds(pl.multiple_of(d * block, block), block)
    out_ref[...] = (total + bias_ref[at][None, :]).astype(BF16)


def image_part_kernel(n_z, which, gain_ref, w_ref, *refs):
    c, z = lax.axis_index("section"), lax.axis_index("mp")
    pieces, (acc_ref, squares_ref) = refs[:-2], refs[-2:]
    rows, block = pieces[0].shape
    acc = jnp.zeros(acc_ref.shape, F32)
    squares = jnp.zeros((rows, 1), F32)
    for (side, k), piece in zip(which, pieces):
        d = (c if side == 0 else 1 - c) * n_z + origin(z, k, n_z)
        at = pl.ds(pl.multiple_of(d * block, block), block)
        x = piece[...].astype(F32)
        squares += jnp.sum(x * x, axis=-1, keepdims=True)
        acc += jnp.dot((x * gain_ref[at][None, :]).astype(BF16), w_ref[at, :], preferred_element_type=F32)
    acc_ref[...] = acc
    squares_ref[...] = jnp.broadcast_to(squares, squares_ref.shape)


def image_keyval_kernel(n_z, which, gain_ref, w_ref, b_ref, acc_ref, squares_ref, *refs):
    pieces, (out_ref, acc, squares) = refs[:-3], refs[-3:]
    image_part_kernel(n_z, which, gain_ref, w_ref, *pieces, acc, squares)
    total = squares[:, :1] + squares_ref[:, :1]
    scale = lax.rsqrt(total * (1.0 / w_ref.shape[0]) + NORM_EPS)
    out_ref[...] = ((acc[...] + acc_ref[...]) * scale + b_ref[...][None, :]).astype(BF16)


def relay_kernel(n_z, linear, *refs):
    z = lax.axis_index("mp")
    pieces, out_ref = refs[:-1], refs[-1]
    if not linear:
        for k, piece in enumerate(pieces):
            out_ref[lax.rem(z - k + n_z, n_z)] = piece[...]
        return
    pair = 1 - 2 * lax.rem(z, 2)
    far = lax.rem(z + 2, n_z)
    for at, piece in zip((z, z + pair, far, far + pair), pieces):
        out_ref[at] = piece[...]


def text_keyval_kernel(gain_ref, w_ref, b_ref, here_ref, there_ref, out_ref):
    c = lax.axis_index("section")
    blocks, rows, model = here_ref.shape
    half = blocks * rows
    acc = jnp.zeros(out_ref.shape, F32)
    squares = jnp.zeros((out_ref.shape[0], 1), F32)
    step = 1024
    for first in range(0, model, step):
        at = slice(first, first + step)
        x = jnp.concatenate([r[i, :, at] for r in (here_ref, there_ref) for i in range(blocks)], axis=0).astype(F32)
        squares += jnp.sum(x * x, axis=-1, keepdims=True)
        y = (x * gain_ref[at][None, :]).astype(BF16)
        acc += jnp.dot(y, w_ref[at, :], preferred_element_type=F32)
    scale = lax.rsqrt(squares * (1.0 / model) + NORM_EPS)
    acc = (acc * scale + b_ref[...][None, :]).astype(BF16)
    out_ref[pl.ds(pl.multiple_of(c * half, half), half), :] = acc[:half]
    out_ref[pl.ds(pl.multiple_of((1 - c) * half, half), half), :] = acc[half:]


def text_place_kernel(n_s, slot_map, place_ref, *refs):
    s = lax.axis_index("seq")
    keyvals, (out_ref, pick_ref, held) = refs[:n_s], refs[n_s:]
    units = place_ref.shape[2]
    group, width = n_s * units, pick_ref.shape[1]
    for k in range(n_s):
        held[lax.rem(s - k + n_s, n_s)] = keyvals[k][...]
    position = lax.broadcasted_iota(jnp.int32, (CTX, units), 0)
    unit = lax.broadcasted_iota(jnp.int32, (units, width), 0)
    lane = lax.broadcasted_iota(jnp.int32, (units, width), 1)

    def source(t):
        def look(n, found):
            return jnp.where(slot_map[n // n_s, n % n_s] == s * n_s + t, n, found)

        found = lax.fori_loop(0, n_s * n_s, look, 0, unroll=n_s == 4)
        return found // n_s, found % n_s

    for t in range(n_s):
        j, i = source(t)
        rows = slice(t * CTX, (t + 1) * CTX)
        chosen = (position == place_ref[i, pl.ds(j, 1), :]).astype(F32)
        covered = jnp.sum(chosen, axis=1, keepdims=True) > 0.5
        text = held[j, pl.ds(pl.multiple_of(i * CTX, CTX), CTX), :]
        out_ref[rows, :] = jnp.where(covered, 0.0, text.astype(F32))
        shift = lax.rem(s - i + n_s, n_s)
        spot = (lane == shift * group + j * units + unit).astype(BF16)
        pick_ref[rows, :] = jnp.dot(chosen.astype(BF16), spot, preferred_element_type=F32).astype(BF16)


def place_kernel(text_ref, pick_ref, *refs):
    keyvals, out_ref = refs[:-1], refs[-1]
    rows = jnp.concatenate([r[...] for r in keyvals], axis=0)
    total = text_ref[...] + jnp.dot(pick_ref[...], rows, preferred_element_type=F32)
    out_ref[...] = total.astype(BF16).reshape(out_ref.shape)


def shards(
    patches,
    image_place,
    slot_map,
    text,
    vision_gain,
    qkv_weight,
    qkv_bias,
    out_weight,
    out_bias,
    merge_gain,
    merge_up,
    merge_up_bias,
    merge_down,
    merge_down_bias,
    input_gain,
    kv_weight,
    kv_bias,
):
    n_z, n_s = lax.axis_size("mp"), lax.axis_size("seq")
    n_d = lax.axis_size("section") * n_z
    x = patches[0]
    rows, width = x.shape
    units = rows // JOIN
    block = rows // n_d
    head_width = out_weight.shape[0]
    model = merge_down.shape[1]
    columns = model // n_d
    kv_width = kv_weight.shape[1]

    def swap(v):
        return lax.ppermute(v, "section", [(0, 1), (1, 0)])

    linear = n_z == 4

    def near(v):
        return lax.ppermute(v, "mp", [(0, 1), (1, 0), (2, 3), (3, 2)])

    def across(v):
        return lax.ppermute(v, "mp", [(0, 2), (2, 0), (1, 3), (3, 1)])

    def spread(own):
        here = [own] + [shifted(own, "mp", n_z, k) for k in range(1, n_z)]
        return here + [swap(v) for v in here]

    text_own = text[0]

    if linear:
        across_own, near_own = across(text_own), near(text_own)
        near_across = near(across_own)
        text_pieces = [text_own, near_own, across_own, near_across]
        early, late = [across_own, near_own], [near_across]
    else:
        text_pieces = [text_own] + [shifted(text_own, "mp", n_z, k) for k in range(1, n_z)]
        early, late = text_pieces[1:2], text_pieces[2:3]

    w = qkv_weight.transpose(1, 2, 0).reshape(3 * head_width, width)
    later = [merge_gain, merge_up.T, merge_up_bias, merge_down_bias, input_gain, kv_bias]
    keep, base, *rest = call(
        functools.partial(front_kernel, n_z, block, len(later)),
        [struct((rows // 2, width), BF16), struct((block, width), F32)]
        + [struct((block, width), BF16)] * n_z
        + [struct(v.shape, v.dtype) for v in later],
        [image_place, x, vision_gain, w, qkv_bias, out_weight, out_bias] + later,
        scratch=[
            pltpu.VMEM((rows, head_width), BF16), pltpu.SMEM(image_place.shape, jnp.int32),
            pltpu.VMEM(x.shape, BF16), pltpu.VMEM(vision_gain.shape, F32), pltpu.VMEM(w.shape, BF16),
            pltpu.VMEM(qkv_bias.shape, F32), pltpu.VMEM(out_weight.shape, BF16), pltpu.VMEM(out_bias.shape, F32),
            pltpu.SemaphoreType.DMA((7 + len(later),)),
        ],
        raw=True,
        grant=24,
        flops=2 * rows * width * 4 * head_width,
    )
    sends, (gain, up, up_bias, down_bias, text_gain, bias) = rest[:n_z], rest[n_z:]
    parts = call(
        functools.partial(pair_rows_kernel, n_z, block),
        [struct((block, width), F32)] + [struct((block, width), BF16)] * (n_z - 1),
        [keep] + [swap(v) for v in sends],
    )
    sums = [parts[0]] + [shifted(parts[k], "mp", n_z, k) for k in range(1, n_z)]
    merged, = call(
        resid_kernel, [struct((block, width), BF16)], [base, gain] + sums, after=early)
    pieces = spread(merged)

    hidden, = call(
        functools.partial(hidden_kernel, n_z, block),
        [struct((units, merge_up.shape[1]), BF16)],
        [up, up_bias] + pieces,
        scratch=[pltpu.VMEM((JOIN, units, width), BF16)],
        flops=2 * units * merge_up.size,
    )
    sends, keeps = (
        call(
            functools.partial(down_kernel, other),
            [struct((units, columns), BF16)] * n_z,
            [hidden, merge_down],
            after=late if other else (),
            flops=units * merge_down.size,
            grant=16,
        )
        for other in (True, False)
    )
    parts = call(
        functools.partial(pair_columns_kernel, n_z),
        [struct((units, columns), F32)] + [struct((units, columns), BF16)] * (n_z - 1),
        [*keeps, *(swap(v) for v in sends)],
    )
    sums = [parts[0]] + [shifted(parts[k], "mp", n_z, k) for k in range(1, n_z)]
    line, = call(
        functools.partial(relay_kernel, n_z, linear), [struct((n_z,) + text_own.shape, BF16)], text_pieces, after=parts[:1])
    prompt = n_d * text.shape[1]
    text_keyval, = call(
        text_keyval_kernel,
        [struct((prompt, kv_width), BF16)],
        [text_gain, kv_weight, bias, line, swap(line)],
        flops=2 * prompt * model * kv_width,
        grant=16,
    )
    texts = [text_keyval] + [shifted(text_keyval, "seq", n_s, k) for k in range(1, n_s)]
    image, = call(
        functools.partial(image_kernel, n_z), [struct((units, columns), BF16)], [down_bias] + sums, after=texts[1:])
    image_pieces = spread(image)

    text_placed, pick = call(
        functools.partial(text_place_kernel, n_s),
        [struct((n_s * CTX, kv_width), F32), struct((n_s * CTX, n_s * units), BF16)],
        [slot_map, image_place] + texts,
        scratch=[pltpu.VMEM((n_s, prompt, kv_width), BF16)],
        smem=1,
        grant=24,
    )

    sides = [(i // n_z, i % n_z) for i in range(2 * n_z)]
    first, last = ([s for s in sides if (s[1] == n_z - 1) == end] for end in (False, True))
    acc, squares = call(
        functools.partial(image_part_kernel, n_z, first),
        [struct((units, kv_width), F32), struct((units, 128), F32)],
        [text_gain, kv_weight] + [image_pieces[side * n_z + k] for side, k in first],
        flops=units * model * kv_width,
        grant=16,
    )
    keyval, = call(
        functools.partial(image_keyval_kernel, n_z, last),
        [struct((units, kv_width), BF16)],
        [text_gain, kv_weight, bias, acc, squares] + [image_pieces[side * n_z + k] for side, k in last],
        scratch=[pltpu.VMEM((units, kv_width), F32), pltpu.VMEM((units, 128), F32)],
        grant=16,
    )
    keyvals = [keyval] + [shifted(keyval, "seq", n_s, k) for k in range(1, n_s)]
    cache, = call(
        place_kernel, [struct((n_s, CTX, kv_width), BF16)], [text_placed, pick] + keyvals, grant=24)
    return cache[None]


def solution(mesh):
    placed = (
        P("seq", None, None),
        P(),
        P(),
        P("seq", ("section", "mp"), None),
        P(),
        P(None, None, ("section", "mp")),
        P(None, ("section", "mp")),
        P(("section", "mp"), None),
        P(),
        P(),
        P(None, ("section", "mp")),
        P(("section", "mp")),
        P(("section", "mp"), None),
        P(),
        P(),
        P(None, ("section", "mp")),
        P(("section", "mp")),
    )
    return jax.shard_map(
        shards,
        mesh=mesh,
        in_specs=placed,
        out_specs=P("section", "seq", None, "mp"),
        check_vma=False,
    )
```
